128 devices in a mesh: section: 8 (over z, y_hi), dp: 16 (over y_lo, x, core).
Axes of the slice: x: 4, y: 4 (y_hi: 2, y_lo: 2; y = y_hi * 2 + y_lo), z: 4, core: 2. Of those that a mesh axis runs over, the one named last changes fastest.
Arguments:
- inputs: bfloat16 [4, 768, 4096], P(None, 'dp'), may hold values from -6 to 6
- cotangent: bfloat16 [4, 768, 4096], P(None, 'dp'), may hold values from -0.119628906 to 0.119628906
- w_in: bfloat16 [2, 8, 4096, 256], P(None, 'section', 'dp'), may hold values from -0.09375 to 0.09375
- w_out: bfloat16 [2, 8, 4096, 256], P(None, 'section', 'dp'), may hold values from -0.375 to 0.375
- norm_gain: bfloat16 [2, 8, 4096], P(None, 'section', 'dp'), may hold values from 0.5 to 1.5
Outputs:
- w_in_grad: float32 [2, 8, 4096, 256], P(None, 'section', 'dp')
- w_out_grad: float32 [2, 8, 4096, 256], P(None, 'section', 'dp')
- gain_grad: float32 [2, 8, 4096], P(None, 'section', 'dp')
The draws below stay inside these ranges and needn't reach their ends.
All inputs are finite; a program needn't handle non-finite values.
Results may differ from the reference program's by a relative error of at most 0.04.
Values may be sent and summed in bfloat16 or wider, within the bound.
No kernel may reach another device: no remote copies, remote signals or barrier semaphores. Data moves between devices by JAX's collectives and lax.ppermute only.
A program may use at most 128 MiB of HBM per device.

```python
import jax
import jax.numpy as jnp
from jax import lax

D = 4096
K = 256
MB = 4
TOKENS = 768
N_SECTION = 8


def raised(result, rng, source, target, shards_of, factor):
    def block_of(dim):
        return (jnp.arange(result.shape[dim]) // (result.shape[dim] // shards_of)).reshape((-1,) + (1,) * (result.ndim - 1 - dim))

    near = jax.random.permutation(rng, shards_of)[block_of(target)]
    other_side = (block_of(target) + shards_of // 2) % shards_of
    return jnp.where((block_of(source) == near) | (block_of(source) == other_side), factor * result, result)


def block_scale(key, dims, split, least, top_value):
    def one(position, blocks):
        heights = jax.random.uniform(jax.random.fold_in(jax.random.fold_in(key, 6), position), (blocks,), jnp.float32, least / len(split), top_value / len(split))
        return jnp.repeat(jnp.exp(heights), dims[position] // blocks).reshape((-1,) + (1,) * (len(dims) - position - 1))

    factor_of = one(*split[0])
    for cut in split[1:]:
        factor_of = factor_of * one(*cut)
    return factor_of


def noise(own_key, extent, scale, bound, shards=(), dtype=jnp.bfloat16):
    loudness = block_scale(own_key, extent, shards, -0.22, 0.18) if shards else 1.0
    drawn = jax.random.normal(own_key, extent, jnp.float32) * scale * loudness
    return jnp.minimum(jnp.maximum(drawn, -bound), bound).astype(dtype)


def heavy_noise(stream_key, dims, width, most, pieces, heavy, kind=jnp.bfloat16):
    values = width * jax.random.normal(stream_key, dims, jnp.float32)
    if pieces:
        values = values * block_scale(stream_key, dims, pieces, -0.22, 0.18)
    return jnp.clip(raised(values, jax.random.fold_in(stream_key, 3), *heavy), -most, most).astype(kind)


def setup_inputs(seed: int = 0) -> dict:
    key_list = jax.random.split(jax.random.key(seed), 6)
    return {
        "inputs": heavy_noise(key_list[0], (MB, TOKENS, D), 1.0, 6.0, ((1, 16),), (1, 2, 16, 2.0)),
        "cotangent": noise(key_list[1], (MB, TOKENS, D), 0.02, 0.119628906, ((1, 16),)),
        "w_in": noise(key_list[2], (2, N_SECTION, D, K), D ** -0.5, 0.09375, ((1, 8), (2, 16))),
        "w_out": noise(key_list[3], (2, N_SECTION, D, K), K ** -0.5, 0.375, ((1, 8), (2, 16))),
        "norm_gain": jnp.clip(1.0 + 0.1 * jax.random.normal(key_list[4], (2, N_SECTION, D), jnp.float32), 0.5, 1.5).astype(jnp.bfloat16),
    }


EPS = 1e-06

def norm_parts(layer_input, norm_gain, w_in):
    widened = layer_input.astype(jnp.float32)
    inv_rms = lax.rsqrt(lax.optimization_barrier(jnp.mean(widened * widened, axis=-1, keepdims=True)) + EPS)
    normed = (widened * inv_rms * norm_gain.astype(jnp.float32)).astype(jnp.bfloat16)
    active = jnp.dot(normed, w_in, preferred_element_type=jnp.float32)
    return (widened, inv_rms, normed, active)

def layer_forward(layer_input, norm_gain, w_in, w_out):
    widened, inv_rms, normed, active = norm_parts(layer_input, norm_gain, w_in)
    lifted = jax.nn.silu(active).astype(jnp.bfloat16)
    branch_out = lax.dot_general(lifted, w_out, (((1,), (1,)), ((), ())), preferred_element_type=jnp.float32)
    return ((widened + branch_out).astype(jnp.bfloat16), normed, active)

def layer_backward(layer_input, normed, active, norm_gain, w_in, w_out, upstream):
    widened = layer_input.astype(jnp.float32)
    inv_rms = lax.rsqrt(lax.optimization_barrier(jnp.mean(widened * widened, axis=-1, keepdims=True)) + EPS)
    lifted = jax.nn.silu(active).astype(jnp.bfloat16)
    grad_lift = jnp.dot(upstream, w_out, preferred_element_type=jnp.float32)
    logistic = jax.nn.sigmoid(active)
    grad_act = (grad_lift * logistic * (1.0 + active * (1.0 - logistic))).astype(jnp.bfloat16)
    grad_norm = lax.dot_general(grad_act, w_in, (((1,), (1,)), ((), ())), preferred_element_type=jnp.float32)
    scaled = grad_norm * norm_gain.astype(jnp.float32)
    inner_mean = lax.optimization_barrier(jnp.mean(widened * scaled, axis=-1, keepdims=True))
    cubed = inv_rms * inv_rms * inv_rms
    grad_input = (upstream.astype(jnp.float32) + inv_rms * scaled - widened * cubed * inner_mean).astype(jnp.bfloat16)
    gain_piece = lax.optimization_barrier(jnp.sum(grad_norm * widened * inv_rms, axis=0))
    return (grad_input, grad_act, lifted, gain_piece)

def reference(inputs, cotangent, w_in, w_out, norm_gain):
    layer_order = [(0, section_index) for section_index in range(N_SECTION)]
    layer_order = layer_order + [(1, section_index) for section_index in range(N_SECTION - 1, -1, -1)]
    grads_in = {}
    grads_out = {}
    grads_gain = {}
    for half_index, section_index in layer_order:
        grads_in[half_index, section_index] = jnp.zeros((D, K), jnp.float32)
        grads_out[half_index, section_index] = jnp.zeros((D, K), jnp.float32)
        grads_gain[half_index, section_index] = jnp.zeros((D,), jnp.float32)
    for micro_index in range(MB):
        stream = inputs[micro_index]
        stash_list = []
        for half_index, section_index in layer_order:
            stash_list.append(stream)
            stream, _, _ = layer_forward(stream, norm_gain[half_index, section_index], w_in[half_index, section_index], w_out[half_index, section_index])
        upstream = cotangent[micro_index]
        for layer_place in range(len(layer_order) - 1, -1, -1):
            half_index, section_index = layer_order[layer_place]
            layer_input = stash_list[layer_place]
            gain_now = norm_gain[half_index, section_index]
            in_now = w_in[half_index, section_index]
            out_now = w_out[half_index, section_index]
            _, _, normed, active = norm_parts(layer_input, gain_now, in_now)
            grad_input, grad_act, lifted, gain_piece = layer_backward(layer_input, normed, active, gain_now, in_now, out_now, upstream)
            place_key = (half_index, section_index)
            grads_in[place_key] = grads_in[place_key] + jnp.dot(normed.T, grad_act, preferred_element_type=jnp.float32)
            grads_out[place_key] = grads_out[place_key] + jnp.dot(upstream.T, lifted, preferred_element_type=jnp.float32)
            grads_gain[place_key] = grads_gain[place_key] + gain_piece
            upstream = grad_input
    w_in_grad = jnp.stack([jnp.stack([grads_in[half_index, section_index] for section_index in range(N_SECTION)]) for half_index in range(2)])
    w_out_grad = jnp.stack([jnp.stack([grads_out[half_index, section_index] for section_index in range(N_SECTION)]) for half_index in range(2)])
    gain_grad = jnp.stack([jnp.stack([grads_gain[half_index, section_index] for section_index in range(N_SECTION)]) for half_index in range(2)])
    return (w_in_grad, w_out_grad, gain_grad)
```

```python
import functools

import jax
import jax.numpy as jnp
from jax import lax
from jax.experimental import pallas as pl
from jax.experimental.pallas import tpu as pltpu
from jax.sharding import Mesh, PartitionSpec as P

EPS = 1e-06
PARTS = 2
STAGES = 4
DEPTH = 4
PLANE = ("yh", "yl", "x", "c")
SPLIT = 2
bf16, f32 = jnp.bfloat16, jnp.float32


def narrow_t(left, right):
    return lax.dot_general(left, right, (((1,), (1,)), ((), ())), preferred_element_type=f32)


def square_mean_inverse(rows):
    return lax.rsqrt(jnp.mean(rows * rows, axis=-1, keepdims=True) + EPS)


def forward_kernel(info, feed, incoming, weights, _, __, outgoing, kept_x, kept_act, xs, acc, inv, lifted):
    step = pl.program_id(0)
    active = info[0] == 1
    part = lax.rem(step, 4)
    half = xs.shape[1] // SPLIT
    block = weights[...].reshape(half, weights.shape[-1])

    @pl.when(jnp.logical_and(active, step == 0))
    def _load():
        first = info[3] == 1

        @pl.when(first)
        def _feed():
            xs[...] = feed[0].astype(f32)

        @pl.when(jnp.logical_not(first))
        def _received():
            xs[...] = incoming[...].astype(f32)

    @pl.when(jnp.logical_and(active, part == 0))
    def _in0():
        rows = xs[...].astype(bf16)
        kept_x[0, 0] = rows
        inv[...] = jnp.broadcast_to(square_mean_inverse(rows.astype(f32)), inv.shape)
        acc[...] = jnp.dot(rows[:, :half], block, preferred_element_type=f32)

    @pl.when(jnp.logical_and(active, part == 1))
    def _in1():
        total = acc[...] + jnp.dot(kept_x[0, 0, :, half:], block, preferred_element_type=f32)
        act = total * inv[:, :1]
        kept_act[0, 0] = act
        lifted[...] = (act * jax.nn.sigmoid(act)).astype(bf16)

    @pl.when(jnp.logical_and(active, part == 2))
    def _out0():
        xs[:, :half] = xs[:, :half] + narrow_t(lifted[...], block)

    @pl.when(jnp.logical_and(active, part == 3))
    def _out1():
        xs[:, half:] = xs[:, half:] + narrow_t(lifted[...], block)

    @pl.when(jnp.logical_and(active, step == 4 * DEPTH - 1))
    def _store():
        outgoing[...] = xs[...].astype(bf16)


def backward_kernel(
    info, feed, incoming, weights, kept_x, kept_act, _, __, ___,
    outgoing, kept_u, kept_h, kept_l, us, acc, coef, narrow,
):
    step = pl.program_id(0)
    active = info[0] == 1
    part = lax.rem(step, 4)
    half = us.shape[1] // SPLIT
    block = weights[...].reshape(half, weights.shape[-1])

    @pl.when(jnp.logical_and(active, step == 0))
    def _load():
        first = info[3] == 1

        @pl.when(first)
        def _feed():
            us[...] = feed[0].astype(f32)

        @pl.when(jnp.logical_not(first))
        def _received():
            us[...] = incoming[...].astype(f32)

    @pl.when(jnp.logical_and(active, part == 0))
    def _out0():
        rows = us[...].astype(bf16)
        kept_u[0, 0] = rows
        acc[...] = jnp.dot(rows[:, :half], block, preferred_element_type=f32)

    @pl.when(jnp.logical_and(active, part == 1))
    def _out1():
        grad_lift = acc[...] + jnp.dot(kept_u[0, 0, :, half:], block, preferred_element_type=f32)
        act = kept_act[0, 0]
        inv = square_mean_inverse(kept_x[0, 0].astype(f32))
        logistic = jax.nn.sigmoid(act)
        grad_act = grad_lift * logistic * (1.0 + act * (1.0 - logistic))
        scaled = (grad_act * inv).astype(bf16)
        narrow[...] = scaled
        kept_h[0, 0] = scaled
        kept_l[0, 0] = (act * logistic).astype(bf16)
        weight = jnp.sum(grad_act * act, axis=-1, keepdims=True) * (inv * inv) * (1.0 / us.shape[1])
        coef[...] = jnp.broadcast_to(weight, coef.shape)

    @pl.when(jnp.logical_and(active, part == 2))
    def _in0():
        us[:, :half] = us[:, :half] + narrow_t(narrow[...], block) - kept_x[0, 0, :, :half].astype(f32) * coef[:, :1]

    @pl.when(jnp.logical_and(active, part == 3))
    def _in1():
        us[:, half:] = us[:, half:] + narrow_t(narrow[...], block) - kept_x[0, 0, :, half:].astype(f32) * coef[:, :1]

    @pl.when(jnp.logical_and(active, step == 4 * DEPTH - 1))
    def _store():
        outgoing[...] = us[...].astype(bf16)


def grads_kernel(info, kept_x, kept_u, kept_h, kept_l, out):
    which = pl.program_id(1)
    rows = kept_x.shape[0] * kept_x.shape[2]

    def product(wide, thin):
        left = wide[...].reshape(rows, wide.shape[-1])
        right = thin[...].reshape(rows, thin.shape[-1])
        made = lax.dot_general(left, right, (((0,), (0,)), ((), ())), preferred_element_type=f32)
        out[...] = made.astype(bf16).reshape(out.shape)

    @pl.when(which == 0)
    def _in():
        product(kept_x, kept_h)

    @pl.when(which == 1)
    def _out():
        product(kept_u, kept_l)


def layer_of(info, place):
    return jnp.where(info[2] == 0, place, DEPTH - 1 - place)


def weight_spec(block_count, per_block, lowrank, forward):
    def index(step, info):
        place = step // 4
        side = lax.rem(step, 4) // 2
        if not forward:
            place, side = DEPTH - 1 - place, 1 - side
        layer = layer_of(info, place)
        spot = (lax.rem(layer, 2), lax.rem(step, SPLIT), layer // 2, side, 0, 0)
        return tuple(jnp.where(info[0] == 1, s, 0) for s in spot)

    return pl.BlockSpec((1, block_count // SPLIT, 1, 1, per_block, lowrank), index)


def place_of(step, forward):
    return step // 4 if forward else DEPTH - 1 - step // 4


def kept_spec(rows, width, forward):
    return pl.BlockSpec((1, 1, rows, width), lambda step, info: (info[1], place_of(step, forward), 0, 0))


def feed_spec(rows, width, parts):
    return pl.BlockSpec((1, rows, width), lambda step, info: (jnp.minimum(info[1], parts - 1), 0, 0))


def whole_spec(rows, width):
    return pl.BlockSpec((rows, width), lambda step, info: (0, 0))


ANY = pl.BlockSpec(memory_space=pl.ANY)


def shape_of(array):
    return jax.ShapeDtypeStruct(array.shape, array.dtype)


def forward_visit(info, feed, incoming, weights, kept_x, kept_act):
    parts, rows, width = feed.shape
    lowrank = weights.shape[-1]
    return pl.pallas_call(
        forward_kernel,
        grid_spec=pltpu.PrefetchScalarGridSpec(
            num_scalar_prefetch=1,
            grid=(4 * DEPTH,),
            in_specs=[
                feed_spec(rows, width, parts),
                whole_spec(rows, width),
                weight_spec(weights.shape[1], weights.shape[-2], lowrank, True),
                ANY,
                ANY,
            ],
            out_specs=[
                whole_spec(rows, width),
                kept_spec(rows, width, True),
                kept_spec(rows, lowrank, True),
            ],
            scratch_shapes=[
                pltpu.VMEM((rows, width), f32),
                pltpu.VMEM((rows, lowrank), f32),
                pltpu.VMEM((rows, 128), f32),
                pltpu.VMEM((rows, lowrank), bf16),
            ],
        ),
        out_shape=[jax.ShapeDtypeStruct((rows, width), bf16), shape_of(kept_x), shape_of(kept_act)],
        input_output_aliases={4: 1, 5: 2},
        compiler_params=pltpu.CompilerParams(vmem_limit_bytes=24 * 1024 * 1024),
        cost_estimate=pl.CostEstimate(flops=2 * DEPTH * 2 * rows * width * lowrank, bytes_accessed=weights.size * 2, transcendentals=0),
        name="forward_visit",
    )(info, feed, incoming, weights, kept_x, kept_act)


def backward_visit(info, feed, incoming, weights, kept_x, kept_act, kept_u, kept_h, kept_l):
    parts, rows, width = feed.shape
    lowrank = weights.shape[-1]
    return pl.pallas_call(
        backward_kernel,
        grid_spec=pltpu.PrefetchScalarGridSpec(
            num_scalar_prefetch=1,
            grid=(4 * DEPTH,),
            in_specs=[
                feed_spec(rows, width, parts),
                whole_spec(rows, width),
                weight_spec(weights.shape[1], weights.shape[-2], lowrank, False),
                kept_spec(rows, width, False),
                kept_spec(rows, lowrank, False),
                ANY,
                ANY,
                ANY,
            ],
            out_specs=[
                whole_spec(rows, width),
                kept_spec(rows, width, False),
                kept_spec(rows, lowrank, False),
                kept_spec(rows, lowrank, False),
            ],
            scratch_shapes=[
                pltpu.VMEM((rows, width), f32),
                pltpu.VMEM((rows, lowrank), f32),
                pltpu.VMEM((rows, 128), f32),
                pltpu.VMEM((rows, lowrank), bf16),
            ],
        ),
        out_shape=[
            jax.ShapeDtypeStruct((rows, width), bf16),
            shape_of(kept_u),
            shape_of(kept_h),
            shape_of(kept_l),
        ],
        input_output_aliases={6: 1, 7: 2, 8: 3},
        compiler_params=pltpu.CompilerParams(vmem_limit_bytes=24 * 1024 * 1024),
        cost_estimate=pl.CostEstimate(flops=2 * DEPTH * 2 * rows * width * lowrank, bytes_accessed=weights.size * 2, transcendentals=0),
        name="backward_visit",
    )(info, feed, incoming, weights, kept_x, kept_act, kept_u, kept_h, kept_l)


def weight_grads(info, kept_x, kept_u, kept_h, kept_l, parts, weights):
    rows, width = kept_x.shape[2:]
    lowrank = kept_h.shape[-1]
    wide = pl.BlockSpec((parts, 1, rows, width // SPLIT), lambda q, io, ch, info: (0, layer_of(info, q), 0, ch))
    thin = pl.BlockSpec((parts, 1, rows, lowrank), lambda q, io, ch, info: (0, layer_of(info, q), 0, 0))
    return pl.pallas_call(
        grads_kernel,
        grid_spec=pltpu.PrefetchScalarGridSpec(
            num_scalar_prefetch=1,
            grid=(DEPTH, 2, SPLIT),
            in_specs=[wide, wide, thin, thin],
            out_specs=pl.BlockSpec(
                (1, weights.shape[1] // SPLIT, 1, 1) + weights.shape[-2:],
                lambda q, io, ch, info: (lax.rem(q, 2), ch, q // 2, io, 0, 0),
            ),
        ),
        out_shape=shape_of(weights),
        compiler_params=pltpu.CompilerParams(vmem_limit_bytes=32 * 1024 * 1024),
        name="weight_grads",
    )(info, kept_x, kept_u, kept_h, kept_l)


def per_device(inputs, cotangent, w_in, w_out, norm_gain):
    batches, tok_rows, features = inputs.shape
    own_rows, lowrank = w_in.shape[2:]
    z, yh = lax.axis_index("z"), lax.axis_index("yh")
    low = lax.rem(z, 2)
    leg = jnp.where(jnp.logical_or(z == 0, z == STAGES - 1), 0, 1)
    stage = lax.rem(STAGES - z, STAGES)
    pairs = [(i, i ^ 1) for i in range(STAGES)]

    gain = norm_gain[:, 0].astype(f32)[:, :, None]
    wide_in = w_in[:, 0].astype(f32)
    both = jnp.stack([(wide_in * gain).astype(bf16), w_out[:, 0]], 1)
    keep = lax.dynamic_index_in_dim(both, leg, 0, keepdims=False)
    other = lax.ppermute(lax.dynamic_index_in_dim(both, 1 - leg, 0, keepdims=False), "z", pairs)
    local = jnp.where(low == 0, jnp.stack([keep, other]), jnp.stack([other, keep]))
    weights = lax.all_gather(local, PLANE, axis=0, tiled=False)
    blocks = weights.shape[0] // 2
    weights = weights.reshape((2, blocks) + weights.shape[1:])

    share = batches // 2 * tok_rows
    rows = share // PARTS

    def mine(array):
        piece = lax.dynamic_slice_in_dim(array, yh * (batches // 2), batches // 2, 0)
        return piece.reshape(PARTS, rows, features)

    feed, cot = mine(inputs), mine(cotangent)
    kept_x = jnp.zeros((PARTS + 1, DEPTH, rows, features), bf16)
    kept_act = jnp.zeros((PARTS + 1, DEPTH, rows, lowrank), f32)
    kept_u = jnp.zeros((PARTS + 1, DEPTH, rows, features), bf16)
    kept_h = jnp.zeros((PARTS + 1, DEPTH, rows, lowrank), bf16)
    kept_l = jnp.zeros((PARTS + 1, DEPTH, rows, lowrank), bf16)

    def info_for(part, first):
        active = jnp.logical_and(part >= 0, part < PARTS)
        return jnp.stack(
            [active.astype(jnp.int32), jnp.where(active, part, PARTS), leg, first.astype(jnp.int32)]
        ).astype(jnp.int32)

    onward = [(z_from, (z_from - 1) % STAGES) for z_from in (0, 3, 2)]
    homeward = [(b, a) for a, b in onward]
    coming, returning = feed[0], cot[0]
    for tick in range(PARTS + 2 * STAGES - 2):
        do_forward = tick < PARTS + STAGES - 1
        do_backward = tick >= STAGES - 1
        if do_forward:
            info = info_for(tick - stage, stage == 0)
            if tick > STAGES - 1:
                info, kept_h = lax.optimization_barrier((info, kept_h))
            coming, kept_x, kept_act = forward_visit(info, feed, coming, weights, kept_x, kept_act)
            if tick < PARTS + STAGES - 2:
                coming = lax.ppermute(coming, "z", onward)
        if do_backward:
            info = info_for(tick - (2 * STAGES - 2) + stage, stage == STAGES - 1)
            returning, kept_u, kept_h, kept_l = backward_visit(
                info, cot, returning, weights, kept_x, kept_act, kept_u, kept_h, kept_l
            )
            if tick < PARTS + 2 * STAGES - 3:
                returning = lax.ppermute(returning, "z", homeward)

    grads = weight_grads(info, kept_x, kept_u, kept_h, kept_l, PARTS, weights)
    grads = grads.reshape((2 * blocks,) + grads.shape[2:])
    owned = lax.psum_scatter(grads, PLANE, scatter_dimension=0, tiled=True)[0]
    kept = lax.dynamic_index_in_dim(owned, low, 0, keepdims=False)
    swapped = lax.ppermute(lax.dynamic_index_in_dim(owned, 1 - low, 0, keepdims=False), "z", pairs)
    legs = jnp.where(leg == 0, jnp.stack([kept, swapped]), jnp.stack([swapped, kept])).astype(f32)
    grad_in = legs[:, 0] * gain
    gain_grad = jnp.sum(legs[:, 0] * wide_in, axis=-1)
    return grad_in[:, None], legs[:, 1][:, None], gain_grad[:, None]


def solution(mesh):
    fine = Mesh(mesh.devices.reshape(STAGES, 2, 2, 4, 2), ("z",) + PLANE)
    sec, dp = ("z", "yh"), ("yl", "x", "c")
    return jax.shard_map(
        per_device,
        mesh=fine,
        in_specs=(
            P(None, dp, None),
            P(None, dp, None),
            P(None, sec, dp, None),
            P(None, sec, dp, None),
            P(None, sec, dp),
        ),
        out_specs=(
            P(None, sec, dp, None),
            P(None, sec, dp, None),
            P(None, sec, dp),
        ),
        check_vma=False,
    )
```

```python
import functools

import jax
import jax.numpy as jnp
from jax import lax
from jax.experimental import pallas as pl
from jax.experimental.pallas import tpu as pltpu
from jax.sharding import Mesh, PartitionSpec as P

EPS = 1e-06
PARTS = 2
STAGES = 4
DEPTH = 4
PLANE = ("yh", "yl", "x", "c")
bf16, f32 = jnp.bfloat16, jnp.float32


def narrow_t(left, right):
    return lax.dot_general(left, right, (((1,), (1,)), ((), ())), preferred_element_type=f32)


def square_mean_inverse(rows):
    return lax.rsqrt(jnp.mean(rows * rows, axis=-1, keepdims=True) + EPS)


def layer_weights(weights, layer, side):
    width = weights.shape[1] * weights.shape[-2]
    return weights[lax.rem(layer, 2), :, layer // 2, side].reshape(width, weights.shape[-1])


def forward_kernel(info, feed, incoming, weights, _, __, outgoing, kept_x, kept_act, stage_x, sems):
    @pl.when(info[0] == 1)
    def _run():
        part = info[1]

        def keep(place):
            return pltpu.make_async_copy(stage_x.at[place], kept_x.at[part, place], sems.at[place])

        xs = jnp.where(info[3] == 1, feed[part], incoming[...]).astype(f32)
        for place in range(DEPTH):
            layer = layer_of(info, place)
            rows = xs.astype(bf16)
            stage_x[place] = rows
            keep(place).start()
            inv = square_mean_inverse(rows.astype(f32))
            act = jnp.dot(rows, layer_weights(weights, layer, 0), preferred_element_type=f32) * inv
            kept_act[part, place] = act
            lifted = (act * jax.nn.sigmoid(act)).astype(bf16)
            xs = xs + narrow_t(lifted, layer_weights(weights, layer, 1))
        outgoing[...] = xs.astype(bf16)
        for place in range(DEPTH):
            keep(place).wait()


def backward_kernel(
    info, feed, incoming, weights, kept_x, kept_act, _, __, ___, outgoing, kept_u, kept_h, kept_l,
    stage_x, stage_u, sems,
):
    @pl.when(info[0] == 1)
    def _run():
        part = info[1]

        def fetch(place):
            return pltpu.make_async_copy(kept_x.at[part, place], stage_x.at[place], sems.at[0, place])

        def keep(place):
            return pltpu.make_async_copy(stage_u.at[place], kept_u.at[part, place], sems.at[1, place])

        for place in reversed(range(DEPTH)):
            fetch(place).start()
        us = jnp.where(info[3] == 1, feed[part], incoming[...]).astype(f32)
        for place in reversed(range(DEPTH)):
            layer = layer_of(info, place)
            rows = us.astype(bf16)
            stage_u[place] = rows
            keep(place).start()
            grad_lift = jnp.dot(rows, layer_weights(weights, layer, 1), preferred_element_type=f32)
            act = kept_act[part, place]
            fetch(place).wait()
            entered = stage_x[place].astype(f32)
            inv = square_mean_inverse(entered)
            logistic = jax.nn.sigmoid(act)
            grad_act = grad_lift * logistic * (1.0 + act * (1.0 - logistic))
            scaled = (grad_act * inv).astype(bf16)
            kept_h[part, place] = scaled
            kept_l[part, place] = (act * logistic).astype(bf16)
            weight = jnp.sum(grad_act * act, axis=-1, keepdims=True) * (inv * inv) * (1.0 / us.shape[1])
            us = us + narrow_t(scaled, layer_weights(weights, layer, 0)) - entered * weight
        outgoing[...] = us.astype(bf16)
        for place in range(DEPTH):
            keep(place).wait()


def grads_kernel(info, wide, thin, out, *, along_x):
    parts, _, rows, _ = wide.shape
    lowrank = thin.shape[-1]
    chips, _, lows, block, _ = out.shape

    def one(at, _):
        outer, inner, low = at // (chips * lows), lax.rem(at // lows, chips), lax.rem(at, lows)
        dx, dy = (outer, inner) if along_x else (inner, outer)
        x, y = lax.rem(info[1] + dx, chips), lax.rem(info[3] + dy, chips)
        place = layer_of(info, lows * low + y // 2)
        column = pl.multiple_of(((lax.rem(y, 2) * chips + x) * 2 + info[0]) * block, block)
        left = wide[:, place, :, pl.ds(column, block)].reshape(parts * rows, block)
        right = thin[:, place].reshape(parts * rows, lowrank)
        made = lax.dot_general(left, right, (((0,), (0,)), ((), ())), preferred_element_type=f32)
        out[outer, inner, low] = made.astype(bf16)
        return 0

    lax.fori_loop(0, chips * chips * lows, one, 0, unroll=4)


def layer_of(info, place):
    return jnp.where(info[2] == 0, place, DEPTH - 1 - place)


SM = pl.BlockSpec(memory_space=pltpu.SMEM)
VM = pl.BlockSpec(memory_space=pltpu.VMEM)
HB = pl.BlockSpec(memory_space=pltpu.HBM)
LIMIT = 20 * 1024 * 1024


def shape_of(array):
    return jax.ShapeDtypeStruct(array.shape, array.dtype)


def cost_of(rows, weights):
    flops = 2 * rows * weights.size
    return pl.CostEstimate(flops=flops, bytes_accessed=weights.size * 4, transcendentals=0)


def staged(rows, width):
    return pltpu.VMEM((DEPTH, rows, width), bf16)


def forward_visit(info, feed, incoming, weights, kept_x, kept_act):
    return pl.pallas_call(
        forward_kernel,
        in_specs=[SM, VM, VM, VM, HB, VM],
        out_specs=[VM, HB, VM],
        scratch_shapes=[staged(*incoming.shape), pltpu.SemaphoreType.DMA((DEPTH,))],
        out_shape=[shape_of(incoming), shape_of(kept_x), shape_of(kept_act)],
        input_output_aliases={4: 1, 5: 2},
        compiler_params=pltpu.CompilerParams(vmem_limit_bytes=LIMIT),
        cost_estimate=cost_of(incoming.shape[0], weights),
        name="forward_visit",
    )(info, feed, incoming, weights, kept_x, kept_act)


def backward_visit(info, feed, incoming, weights, kept_x, kept_act, kept_u, kept_h, kept_l):
    return pl.pallas_call(
        backward_kernel,
        in_specs=[SM, VM, VM, VM, HB, VM, HB, VM, VM],
        out_specs=[VM, HB, VM, VM],
        scratch_shapes=[staged(*incoming.shape), staged(*incoming.shape), pltpu.SemaphoreType.DMA((2, DEPTH))],
        out_shape=[shape_of(incoming), shape_of(kept_u), shape_of(kept_h), shape_of(kept_l)],
        input_output_aliases={6: 1, 7: 2, 8: 3},
        compiler_params=pltpu.CompilerParams(vmem_limit_bytes=LIMIT),
        cost_estimate=cost_of(incoming.shape[0], weights),
        name="backward_visit",
    )(info, feed, incoming, weights, kept_x, kept_act, kept_u, kept_h, kept_l)


def weight_grads(info, wide, thin, block, along_x):
    shape = (STAGES, STAGES, 2, block, thin.shape[-1])
    flops = 2 * wide.size // DEPTH * thin.shape[-1] * 2
    return pl.pallas_call(
        functools.partial(grads_kernel, along_x=along_x),
        in_specs=[SM, VM, VM],
        out_specs=VM,
        out_shape=jax.ShapeDtypeStruct(shape, bf16),
        compiler_params=pltpu.CompilerParams(vmem_limit_bytes=LIMIT),
        cost_estimate=pl.CostEstimate(flops=flops, bytes_accessed=wide.size * 4, transcendentals=0),
        name="grads_x" if along_x else "grads_y",
    )(info, wide, thin)


def ring(value, axes, steps):
    return lax.ppermute(value, axes, [(i, (i + steps) % STAGES) for i in range(STAGES)])


def ring_scatter(pieces, axes):
    arrived = [pieces[0]] + [ring(pieces[d], axes, d) for d in range(1, STAGES)]
    return sum(piece.astype(f32) for piece in arrived).astype(bf16)


def per_device(inputs, cotangent, w_in, w_out, norm_gain):
    batches, tok_rows, features = inputs.shape
    own_rows, lowrank = w_in.shape[2:]
    z, yh = lax.axis_index("z"), lax.axis_index("yh")
    low = lax.rem(z, 2)
    leg = jnp.where(jnp.logical_or(z == 0, z == STAGES - 1), 0, 1)
    stage = lax.rem(STAGES - z, STAGES)
    pairs = [(i, i ^ 1) for i in range(STAGES)]

    gain = norm_gain[:, 0].astype(f32)[:, :, None]
    wide_in = w_in[:, 0].astype(f32)
    both = jnp.stack([(wide_in * gain).astype(bf16), w_out[:, 0]], 1)
    keep = lax.dynamic_index_in_dim(both, leg, 0, keepdims=False)
    other = lax.ppermute(lax.dynamic_index_in_dim(both, 1 - leg, 0, keepdims=False), "z", pairs)
    local = jnp.where(low == 0, jnp.stack([keep, other]), jnp.stack([other, keep]))
    weights = lax.all_gather(local, PLANE, axis=0, tiled=False)
    blocks = weights.shape[0] // 2
    weights = weights.reshape((2, blocks) + weights.shape[1:])

    share = batches // 2 * tok_rows
    rows = share // PARTS

    def mine(array):
        piece = lax.dynamic_slice_in_dim(array, yh * (batches // 2), batches // 2, 0)
        return piece.reshape(PARTS, rows, features)

    feed, cot = mine(inputs), mine(cotangent)
    kept_x = jnp.zeros((PARTS, DEPTH, rows, features), bf16)
    kept_act = jnp.zeros((PARTS, DEPTH, rows, lowrank), f32)
    kept_u = jnp.zeros((PARTS, DEPTH, rows, features), bf16)
    kept_h = jnp.zeros((PARTS, DEPTH, rows, lowrank), bf16)
    kept_l = jnp.zeros((PARTS, DEPTH, rows, lowrank), bf16)

    def info_for(part, first):
        active = jnp.logical_and(part >= 0, part < PARTS)
        return jnp.stack(
            [active.astype(jnp.int32), jnp.clip(part, 0, PARTS - 1), leg, first.astype(jnp.int32)]
        ).astype(jnp.int32)

    onward = [(z_from, (z_from - 1) % STAGES) for z_from in (0, 3, 2)]
    homeward = [(b, a) for a, b in onward]
    coming, returning = feed[0], cot[0]
    for tick in range(PARTS + 2 * STAGES - 2):
        do_forward = tick < PARTS + STAGES - 1
        do_backward = tick >= STAGES - 1
        if do_forward:
            info = info_for(tick - stage, stage == 0)
            if tick > STAGES - 1:
                info, kept_h = lax.optimization_barrier((info, kept_h))
            coming, kept_x, kept_act = forward_visit(info, feed, coming, weights, kept_x, kept_act)
            if tick < PARTS + STAGES - 2:
                coming = lax.ppermute(coming, "z", onward)
        if do_backward:
            info = info_for(tick - (2 * STAGES - 2) + stage, stage == STAGES - 1)
            returning, kept_u, kept_h, kept_l = backward_visit(
                info, cot, returning, weights, kept_x, kept_act, kept_u, kept_h, kept_l
            )
            if tick < PARTS + 2 * STAGES - 3:
                returning = lax.ppermute(returning, "z", homeward)

    core, x_here = lax.axis_index("c"), lax.axis_index("x")
    y_here = 2 * yh + lax.axis_index("yl")

    def reduced(wide, thin, along_x):
        def made(which):
            info = jnp.stack([which, x_here, leg, y_here]).astype(jnp.int32)
            return weight_grads(info, wide, thin, own_rows, along_x)

        theirs = lax.ppermute(made(1 - core), "c", [(0, 1), (1, 0)])
        ours = made(core)
        sums = [(ours[d].astype(f32) + theirs[d].astype(f32)).astype(bf16) for d in range(STAGES)]
        order = ("x", ("yh", "yl")) if along_x else (("yh", "yl"), "x")
        return ring_scatter(ring_scatter(sums, order[0]), order[1])

    owned = jnp.stack([reduced(kept_x, kept_h, True), reduced(kept_u, kept_l, False)], 1)
    kept = lax.dynamic_index_in_dim(owned, low, 0, keepdims=False)
    swapped = lax.ppermute(lax.dynamic_index_in_dim(owned, 1 - low, 0, keepdims=False), "z", pairs)
    legs = jnp.where(leg == 0, jnp.stack([kept, swapped]), jnp.stack([swapped, kept])).astype(f32)
    grad_in = legs[:, 0] * gain
    gain_grad = jnp.sum(legs[:, 0] * wide_in, axis=-1)
    return grad_in[:, None], legs[:, 1][:, None], gain_grad[:, None]


def solution(mesh):
    fine = Mesh(mesh.devices.reshape(STAGES, 2, 2, 4, 2), ("z",) + PLANE)
    sec, dp = ("z", "yh"), ("yl", "x", "c")
    return jax.shard_map(
        per_device,
        mesh=fine,
        in_specs=(
            P(None, dp, None),
            P(None, dp, None),
            P(None, sec, dp, None),
            P(None, sec, dp, None),
            P(None, sec, dp),
        ),
        out_specs=(
            P(None, sec, dp, None),
            P(None, sec, dp, None),
            P(None, sec, dp),
        ),
        check_vma=False,
    )
```

```python
import functools

import jax
import jax.numpy as jnp
from jax import lax
from jax.experimental import pallas as pl
from jax.experimental.pallas import tpu as pltpu
from jax.sharding import Mesh, PartitionSpec as P

EPS = 1e-06
PARTS = 2
STAGES = 4
DEPTH = 4
PLANE = ("yh", "yl", "x", "c")
bf16, f32 = jnp.bfloat16, jnp.float32


def narrow_t(left, right):
    return lax.dot_general(left, right, (((1,), (1,)), ((), ())), preferred_element_type=f32)


def square_mean_inverse(rows):
    return lax.rsqrt(jnp.mean(rows * rows, axis=-1, keepdims=True) + EPS)


def layer_weights(weights, layer, side):
    width = weights.shape[1] * weights.shape[-2]
    return weights[lax.rem(layer, 2), :, layer // 2, side].reshape(width, weights.shape[-1])


def forward_kernel(
    table, feed, incoming, weights, _, __, outgoing, kept_x, kept_act, stage_x, sems, *, row
):
    info = [table[row, i] for i in range(4)]

    @pl.when(info[0] == 1)
    def _run():
        part = info[1]

        def keep(place):
            return pltpu.make_async_copy(stage_x.at[place], kept_x.at[part, place], sems.at[place])

        xs = jnp.where(info[3] == 1, feed[part], incoming[...]).astype(f32)
        for place in range(DEPTH):
            layer = layer_of(info, place)
            rows = xs.astype(bf16)
            stage_x[place] = rows
            keep(place).start()
            inv = square_mean_inverse(rows.astype(f32))
            act = jnp.dot(rows, layer_weights(weights, layer, 0), preferred_element_type=f32) * inv
            kept_act[part, place] = act
            lifted = (act * jax.nn.sigmoid(act)).astype(bf16)
            xs = xs + narrow_t(lifted, layer_weights(weights, layer, 1))
        outgoing[...] = xs.astype(bf16)
        for place in range(DEPTH):
            keep(place).wait()


def backward_kernel(
    table, feed, incoming, weights, kept_x, kept_act, _, __, ___, outgoing, kept_u, kept_h, kept_l,
    stage_x, stage_u, sems, *, row,
):
    info = [table[row, i] for i in range(4)]

    @pl.when(info[0] == 1)
    def _run():
        part = info[1]

        def fetch(place):
            return pltpu.make_async_copy(kept_x.at[part, place], stage_x.at[place], sems.at[0, place])

        def keep(place):
            return pltpu.make_async_copy(stage_u.at[place], kept_u.at[part, place], sems.at[1, place])

        for place in reversed(range(DEPTH)):
            fetch(place).start()
        us = jnp.where(info[3] == 1, feed[part], incoming[...]).astype(f32)
        for place in reversed(range(DEPTH)):
            layer = layer_of(info, place)
            rows = us.astype(bf16)
            stage_u[place] = rows
            keep(place).start()
            grad_lift = jnp.dot(rows, layer_weights(weights, layer, 1), preferred_element_type=f32)
            act = kept_act[part, place]
            fetch(place).wait()
            entered = stage_x[place].astype(f32)
            inv = square_mean_inverse(entered)
            logistic = jax.nn.sigmoid(act)
            grad_act = grad_lift * logistic * (1.0 + act * (1.0 - logistic))
            scaled = (grad_act * inv).astype(bf16)
            kept_h[part, place] = scaled
            kept_l[part, place] = (act * logistic).astype(bf16)
            weight = jnp.sum(grad_act * act, axis=-1, keepdims=True) * (inv * inv) * (1.0 / us.shape[1])
            us = us + narrow_t(scaled, layer_weights(weights, layer, 0)) - entered * weight
        outgoing[...] = us.astype(bf16)
        for place in range(DEPTH):
            keep(place).wait()


def grads_kernel(table, wide, thin, out, *, along_x, row):
    info = [table[row, i] for i in range(4)]
    parts, _, rows, _ = wide.shape
    lowrank = thin.shape[-1]
    chips, _, lows, block, _ = out.shape

    def one(at, _):
        outer, inner, low = at // (chips * lows), lax.rem(at // lows, chips), lax.rem(at, lows)
        dx, dy = (outer, inner) if along_x else (inner, outer)
        x, y = lax.rem(info[1] + dx, chips), lax.rem(info[3] + dy, chips)
        place = layer_of(info, lows * low + y // 2)
        column = pl.multiple_of(((lax.rem(y, 2) * chips + x) * 2 + info[0]) * block, block)
        left = wide[:, place, :, pl.ds(column, block)].reshape(parts * rows, block)
        right = thin[:, place].reshape(parts * rows, lowrank)
        made = lax.dot_general(left, right, (((0,), (0,)), ((), ())), preferred_element_type=f32)
        out[outer, inner, low] = made.astype(bf16)
        return 0

    lax.fori_loop(0, chips * chips * lows, one, 0, unroll=4)


def layer_of(info, place):
    return jnp.where(info[2] == 0, place, DEPTH - 1 - place)


SM = pl.BlockSpec(memory_space=pltpu.SMEM)
VM = pl.BlockSpec(memory_space=pltpu.VMEM)
ANY = pl.BlockSpec(memory_space=pl.ANY)
LIMIT = 12 * 1024 * 1024


def shape_of(array):
    return jax.ShapeDtypeStruct(array.shape, array.dtype)


def cost_of(rows, weights):
    flops = 2 * rows * weights.size
    return pl.CostEstimate(flops=flops, bytes_accessed=weights.size * 4, transcendentals=0)


def staged(rows, width):
    return pltpu.VMEM((DEPTH, rows, width), bf16)


def place_kernel(table, source, inputs, cotangent, out, feed, cot, *rest):
    sems = rest[-1]
    pieces, parts = source.shape[0], feed.shape[0]
    start = table[0, 4] * parts
    copies = [
        pltpu.make_async_copy(inputs.at[pl.ds(start, parts)], feed, sems.at[pieces]),
        pltpu.make_async_copy(cotangent.at[pl.ds(start, parts)], cot, sems.at[pieces + 1]),
    ]
    copies += [pltpu.make_async_copy(source.at[i], out.at[i], sems.at[i]) for i in range(pieces)]
    for copy in copies:
        copy.start()
    for copy in copies:
        copy.wait()


def place(table, weights, inputs, cotangent):
    rows, width = inputs.shape[1:]
    lowrank = weights.shape[-1]
    fed = jax.ShapeDtypeStruct((PARTS, rows, width), bf16)
    stream = jax.ShapeDtypeStruct((rows, width), bf16)
    wide = jax.ShapeDtypeStruct((PARTS, DEPTH, rows, width), bf16)
    thin = jax.ShapeDtypeStruct((PARTS, DEPTH, rows, lowrank), bf16)
    acts = jax.ShapeDtypeStruct((PARTS, DEPTH, rows, lowrank), f32)
    shapes = [shape_of(weights), fed, fed, stream, stream, wide, acts, wide, thin, thin]
    return pl.pallas_call(
        place_kernel,
        in_specs=[SM, ANY, ANY, ANY],
        out_specs=[VM] * len(shapes),
        out_shape=shapes,
        scratch_shapes=[pltpu.SemaphoreType.DMA((weights.shape[0] + 2,))],
        compiler_params=pltpu.CompilerParams(vmem_limit_bytes=LIMIT),
        cost_estimate=pl.CostEstimate(flops=0, bytes_accessed=weights.size * 4, transcendentals=0),
        name="place",
    )(table, weights, inputs, cotangent)


def forward_visit(row, table, feed, incoming, weights, kept_x, kept_act):
    return pl.pallas_call(
        functools.partial(forward_kernel, row=row),
        in_specs=[SM, VM, VM, VM, VM, VM],
        out_specs=[VM, VM, VM],
        scratch_shapes=[staged(*incoming.shape), pltpu.SemaphoreType.DMA((DEPTH,))],
        out_shape=[shape_of(incoming), shape_of(kept_x), shape_of(kept_act)],
        input_output_aliases={4: 1, 5: 2},
        compiler_params=pltpu.CompilerParams(vmem_limit_bytes=LIMIT),
        cost_estimate=cost_of(incoming.shape[0], weights),
        name="forward_visit",
    )(table, feed, incoming, weights, kept_x, kept_act)


def backward_visit(row, table, feed, incoming, weights, kept_x, kept_act, kept_u, kept_h, kept_l):
    return pl.pallas_call(
        functools.partial(backward_kernel, row=row),
        in_specs=[SM, VM, VM, VM, VM, VM, VM, VM, VM],
        out_specs=[VM, VM, VM, VM],
        scratch_shapes=[staged(*incoming.shape), staged(*incoming.shape), pltpu.SemaphoreType.DMA((2, DEPTH))],
        out_shape=[shape_of(incoming), shape_of(kept_u), shape_of(kept_h), shape_of(kept_l)],
        input_output_aliases={6: 1, 7: 2, 8: 3},
        compiler_params=pltpu.CompilerParams(vmem_limit_bytes=LIMIT),
        cost_estimate=cost_of(incoming.shape[0], weights),
        name="backward_visit",
    )(table, feed, incoming, weights, kept_x, kept_act, kept_u, kept_h, kept_l)


def weight_grads(row, table, wide, thin, block, along_x):
    shape = (STAGES, STAGES, 2, block, thin.shape[-1])
    flops = 2 * wide.size // DEPTH * thin.shape[-1] * 2
    return pl.pallas_call(
        functools.partial(grads_kernel, along_x=along_x, row=row),
        in_specs=[SM, VM, VM],
        out_specs=VM,
        out_shape=jax.ShapeDtypeStruct(shape, bf16),
        compiler_params=pltpu.CompilerParams(vmem_limit_bytes=LIMIT),
        cost_estimate=pl.CostEstimate(flops=flops, bytes_accessed=wide.size * 4, transcendentals=0),
        name="grads_x" if along_x else "grads_y",
    )(table, wide, thin)


def ring(value, axes, steps):
    return lax.ppermute(value, axes, [(i, (i + steps) % STAGES) for i in range(STAGES)])


def ring_scatter(pieces, axes):
    arrived = [pieces[0]] + [ring(pieces[d], axes, d) for d in range(1, STAGES)]
    return sum(piece.astype(f32) for piece in arrived).astype(bf16)


def per_device(inputs, cotangent, w_in, w_out, norm_gain):
    batches, tok_rows, features = inputs.shape
    own_rows, lowrank = w_in.shape[2:]
    z, yh = lax.axis_index("z"), lax.axis_index("yh")
    low = lax.rem(z, 2)
    leg = jnp.where(jnp.logical_or(z == 0, z == STAGES - 1), 0, 1)
    stage = lax.rem(STAGES - z, STAGES)
    pairs = [(i, i ^ 1) for i in range(STAGES)]

    gain = norm_gain[:, 0].astype(f32)[:, :, None]
    wide_in = w_in[:, 0].astype(f32)
    both = jnp.stack([(wide_in * gain).astype(bf16), w_out[:, 0]], 1)
    keep = lax.dynamic_index_in_dim(both, leg, 0, keepdims=False)
    other = lax.ppermute(lax.dynamic_index_in_dim(both, 1 - leg, 0, keepdims=False), "z", pairs)
    local = jnp.where(low == 0, jnp.stack([keep, other]), jnp.stack([other, keep]))
    gathered = lax.all_gather(local, PLANE, axis=0, tiled=False)
    core, x_here = lax.axis_index("c"), lax.axis_index("x")
    y_here = 2 * yh + lax.axis_index("yl")
    ticks = PARTS + 2 * STAGES - 2
    moments = jnp.arange(ticks, dtype=jnp.int32)

    def rows_for(part, first):
        active = jnp.logical_and(part >= 0, part < PARTS)
        fixed = jnp.stack([leg, first, yh]).astype(jnp.int32)
        moving = jnp.stack([active.astype(jnp.int32), jnp.clip(part, 0, PARTS - 1)], 1)
        return jnp.concatenate([moving, jnp.broadcast_to(fixed, (ticks, 3))], 1)

    table = jnp.concatenate(
        [
            rows_for(moments - stage, stage == 0),
            rows_for(moments - (2 * STAGES - 2) + stage, stage == STAGES - 1),
            jnp.stack([1 - core, x_here, leg, y_here, yh])[None],
            jnp.stack([core, x_here, leg, y_here, yh])[None],
        ]
    ).astype(jnp.int32)
    weights, feed, cot, coming, returning, kept_x, kept_act, kept_u, kept_h, kept_l = place(
        table, gathered, inputs, cotangent
    )
    weights = weights.reshape((2, weights.shape[0] // 2) + weights.shape[1:])

    onward = [(z_from, (z_from - 1) % STAGES) for z_from in (0, 3, 2)]
    homeward = [(b, a) for a, b in onward]
    for tick in range(ticks):
        do_forward = tick < PARTS + STAGES - 1
        do_backward = tick >= STAGES - 1
        if do_forward:
            if tick > STAGES - 1:
                coming, kept_h = lax.optimization_barrier((coming, kept_h))
            coming, kept_x, kept_act = forward_visit(tick, table, feed, coming, weights, kept_x, kept_act)
            if tick < PARTS + STAGES - 2:
                coming = lax.ppermute(coming, "z", onward)
        if do_backward:
            returning, kept_u, kept_h, kept_l = backward_visit(
                ticks + tick, table, cot, returning, weights, kept_x, kept_act, kept_u, kept_h, kept_l
            )
            if tick < PARTS + 2 * STAGES - 3:
                returning = lax.ppermute(returning, "z", homeward)

    def reduced(wide, thin, along_x):
        theirs = lax.ppermute(
            weight_grads(2 * ticks, table, wide, thin, own_rows, along_x), "c", [(0, 1), (1, 0)]
        )
        ours = weight_grads(2 * ticks + 1, table, wide, thin, own_rows, along_x)
        sums = [(ours[d].astype(f32) + theirs[d].astype(f32)).astype(bf16) for d in range(STAGES)]
        order = ("x", ("yh", "yl")) if along_x else (("yh", "yl"), "x")
        return ring_scatter(ring_scatter(sums, order[0]), order[1])

    owned = jnp.stack([reduced(kept_x, kept_h, True), reduced(kept_u, kept_l, False)], 1)
    kept = lax.dynamic_index_in_dim(owned, low, 0, keepdims=False)
    swapped = lax.ppermute(lax.dynamic_index_in_dim(owned, 1 - low, 0, keepdims=False), "z", pairs)
    legs = jnp.where(leg == 0, jnp.stack([kept, swapped]), jnp.stack([swapped, kept])).astype(f32)
    grad_in = legs[:, 0] * gain
    gain_grad = jnp.sum(legs[:, 0] * wide_in, axis=-1)
    return grad_in[:, None], legs[:, 1][:, None], gain_grad[:, None]


def solution(mesh):
    fine = Mesh(mesh.devices.reshape(STAGES, 2, 2, 4, 2), ("z",) + PLANE)
    sec, dp = ("z", "yh"), ("yl", "x", "c")
    return jax.shard_map(
        per_device,
        mesh=fine,
        in_specs=(
            P(None, dp, None),
            P(None, dp, None),
            P(None, sec, dp, None),
            P(None, sec, dp, None),
            P(None, sec, dp),
        ),
        out_specs=(
            P(None, sec, dp, None),
            P(None, sec, dp, None),
            P(None, sec, dp),
        ),
        check_vma=False,
    )
```

```python
import functools

import jax
import jax.numpy as jnp
from jax import lax
from jax.experimental import pallas as pl
from jax.experimental.pallas import tpu as pltpu
from jax.sharding import Mesh, PartitionSpec as P

EPS = 1e-06
PARTS = 2
STAGES = 4
DEPTH = 4
PLANE = ("yh", "yl", "x", "c")
bf16, f32 = jnp.bfloat16, jnp.float32


def narrow_t(left, right):
    return lax.dot_general(left, right, (((1,), (1,)), ((), ())), preferred_element_type=f32)


def square_mean_inverse(rows):
    return lax.rsqrt(jnp.mean(rows * rows, axis=-1, keepdims=True) + EPS)


def layer_weights(weights, layer, side):
    width = weights.shape[1] * weights.shape[-2]
    return weights[lax.rem(layer, 2), :, layer // 2, side].reshape(width, weights.shape[-1])


def forward_kernel(
    table, feed, incoming, weights, _, __, outgoing, kept_x, kept_act, stage_x, sems, *, row
):
    info = [table[row, i] for i in range(4)]

    @pl.when(info[0] == 1)
    def _run():
        part = info[1]

        def keep(place):
            return pltpu.make_async_copy(stage_x.at[place], kept_x.at[part, place], sems.at[place])

        xs = jnp.where(info[3] == 1, feed[part], incoming[...]).astype(f32)
        for place in range(DEPTH):
            layer = layer_of(info, place)
            rows = xs.astype(bf16)
            stage_x[place] = rows
            keep(place).start()
            inv = square_mean_inverse(rows.astype(f32))
            act = jnp.dot(rows, layer_weights(weights, layer, 0), preferred_element_type=f32) * inv
            kept_act[part, place] = act
            lifted = (act * jax.nn.sigmoid(act)).astype(bf16)
            xs = xs + narrow_t(lifted, layer_weights(weights, layer, 1))
        outgoing[...] = xs.astype(bf16)
        for place in range(DEPTH):
            keep(place).wait()


def backward_kernel(
    table, feed, incoming, weights, kept_x, kept_act, _, __, ___, outgoing, kept_u, kept_h, kept_l,
    stage_x, stage_u, sems, *, row,
):
    info = [table[row, i] for i in range(4)]

    @pl.when(info[0] == 1)
    def _run():
        part = info[1]

        def fetch(place):
            return pltpu.make_async_copy(kept_x.at[part, place], stage_x.at[place], sems.at[0, place])

        def keep(place):
            return pltpu.make_async_copy(stage_u.at[place], kept_u.at[part, place], sems.at[1, place])

        for place in reversed(range(DEPTH)):
            fetch(place).start()
        us = jnp.where(info[3] == 1, feed[part], incoming[...]).astype(f32)
        for place in reversed(range(DEPTH)):
            layer = layer_of(info, place)
            rows = us.astype(bf16)
            stage_u[place] = rows
            keep(place).start()
            grad_lift = jnp.dot(rows, layer_weights(weights, layer, 1), preferred_element_type=f32)
            act = kept_act[part, place]
            fetch(place).wait()
            entered = stage_x[place].astype(f32)
            inv = square_mean_inverse(entered)
            logistic = jax.nn.sigmoid(act)
            grad_act = grad_lift * logistic * (1.0 + act * (1.0 - logistic))
            scaled = (grad_act * inv).astype(bf16)
            kept_h[part, place] = scaled
            kept_l[part, place] = (act * logistic).astype(bf16)
            weight = jnp.sum(grad_act * act, axis=-1, keepdims=True) * (inv * inv) * (1.0 / us.shape[1])
            us = us + narrow_t(scaled, layer_weights(weights, layer, 0)) - entered * weight
        outgoing[...] = us.astype(bf16)
        for place in range(DEPTH):
            keep(place).wait()


def grads_kernel(table, wide, thin, out, *, along_x, row):
    info = [table[row, i] for i in range(4)]
    parts, _, rows, _ = wide.shape
    lowrank = thin.shape[-1]
    chips, _, lows, block, _ = out.shape

    def one(at, _):
        outer, inner, low = at // (chips * lows), lax.rem(at // lows, chips), lax.rem(at, lows)
        dx, dy = (outer, inner) if along_x else (inner, outer)
        x, y = lax.rem(info[1] + dx, chips), lax.rem(info[3] + dy, chips)
        place = layer_of(info, lows * low + y // 2)
        column = pl.multiple_of(((lax.rem(y, 2) * chips + x) * 2 + info[0]) * block, block)
        left = wide[:, place, :, pl.ds(column, block)].reshape(parts * rows, block)
        right = thin[:, place].reshape(parts * rows, lowrank)
        made = lax.dot_general(left, right, (((0,), (0,)), ((), ())), preferred_element_type=f32)
        out[outer, inner, low] = made.astype(bf16)
        return 0

    lax.fori_loop(0, chips * chips * lows, one, 0, unroll=4)


def layer_of(info, place):
    return jnp.where(info[2] == 0, place, DEPTH - 1 - place)


SM = pl.BlockSpec(memory_space=pltpu.SMEM)
VM = pl.BlockSpec(memory_space=pltpu.VMEM)
ANY = pl.BlockSpec(memory_space=pl.ANY)
LIMIT = 12 * 1024 * 1024


def shape_of(array):
    return jax.ShapeDtypeStruct(array.shape, array.dtype)


def cost_of(rows, weights):
    flops = 2 * rows * weights.size
    return pl.CostEstimate(flops=flops, bytes_accessed=weights.size * 4, transcendentals=0)


def staged(rows, width):
    return pltpu.VMEM((DEPTH, rows, width), bf16)


def place_kernel(table, source, inputs, cotangent, out, feed, cot, *rest):
    sems = rest[-1]
    pieces, parts = source.shape[0], feed.shape[0]
    start = table[0, 4] * parts
    copies = [
        pltpu.make_async_copy(inputs.at[pl.ds(start, parts)], feed, sems.at[pieces]),
        pltpu.make_async_copy(cotangent.at[pl.ds(start, parts)], cot, sems.at[pieces + 1]),
    ]
    copies += [pltpu.make_async_copy(source.at[i], out.at[i], sems.at[i]) for i in range(pieces)]
    for copy in copies:
        copy.start()
    for copy in copies:
        copy.wait()


def place(table, weights, inputs, cotangent):
    rows, width = inputs.shape[1:]
    lowrank = weights.shape[-1]
    fed = jax.ShapeDtypeStruct((PARTS, rows, width), bf16)
    stream = jax.ShapeDtypeStruct((rows, width), bf16)
    wide = jax.ShapeDtypeStruct((PARTS, DEPTH, rows, width), bf16)
    thin = jax.ShapeDtypeStruct((PARTS, DEPTH, rows, lowrank), bf16)
    acts = jax.ShapeDtypeStruct((PARTS, DEPTH, rows, lowrank), f32)
    shapes = [shape_of(weights), fed, fed, stream, stream, wide, acts, wide, thin, thin]
    return pl.pallas_call(
        place_kernel,
        in_specs=[SM, ANY, ANY, ANY],
        out_specs=[VM] * len(shapes),
        out_shape=shapes,
        scratch_shapes=[pltpu.SemaphoreType.DMA((weights.shape[0] + 2,))],
        compiler_params=pltpu.CompilerParams(vmem_limit_bytes=LIMIT),
        cost_estimate=pl.CostEstimate(flops=0, bytes_accessed=weights.size * 4, transcendentals=0),
        name="place",
    )(table, weights, inputs, cotangent)


def forward_visit(row, table, feed, incoming, weights, kept_x, kept_act):
    return pl.pallas_call(
        functools.partial(forward_kernel, row=row),
        in_specs=[SM, VM, VM, VM, VM, VM],
        out_specs=[VM, VM, VM],
        scratch_shapes=[staged(*incoming.shape), pltpu.SemaphoreType.DMA((DEPTH,))],
        out_shape=[shape_of(incoming), shape_of(kept_x), shape_of(kept_act)],
        input_output_aliases={4: 1, 5: 2},
        compiler_params=pltpu.CompilerParams(vmem_limit_bytes=LIMIT),
        cost_estimate=cost_of(incoming.shape[0], weights),
        name="forward_visit",
    )(table, feed, incoming, weights, kept_x, kept_act)


def backward_visit(row, table, feed, incoming, weights, kept_x, kept_act, kept_u, kept_h, kept_l):
    return pl.pallas_call(
        functools.partial(backward_kernel, row=row),
        in_specs=[SM, VM, VM, VM, VM, VM, VM, VM, VM],
        out_specs=[VM, VM, VM, VM],
        scratch_shapes=[staged(*incoming.shape), staged(*incoming.shape), pltpu.SemaphoreType.DMA((2, DEPTH))],
        out_shape=[shape_of(incoming), shape_of(kept_u), shape_of(kept_h), shape_of(kept_l)],
        input_output_aliases={6: 1, 7: 2, 8: 3},
        compiler_params=pltpu.CompilerParams(vmem_limit_bytes=LIMIT),
        cost_estimate=cost_of(incoming.shape[0], weights),
        name="backward_visit",
    )(table, feed, incoming, weights, kept_x, kept_act, kept_u, kept_h, kept_l)


def weight_grads(row, table, wide, thin, block, along_x):
    shape = (STAGES, STAGES, 2, block, thin.shape[-1])
    flops = 2 * wide.size // DEPTH * thin.shape[-1] * 2
    return pl.pallas_call(
        functools.partial(grads_kernel, along_x=along_x, row=row),
        in_specs=[SM, VM, VM],
        out_specs=VM,
        out_shape=jax.ShapeDtypeStruct(shape, bf16),
        compiler_params=pltpu.CompilerParams(vmem_limit_bytes=LIMIT),
        cost_estimate=pl.CostEstimate(flops=flops, bytes_accessed=wide.size * 4, transcendentals=0),
        name="grads_x" if along_x else "grads_y",
    )(table, wide, thin)


def ring(value, axes, steps):
    return lax.ppermute(value, axes, [(i, (i + steps) % STAGES) for i in range(STAGES)])


def ring_scatter(pieces, axes):
    arrived = [pieces[0]] + [ring(pieces[d], axes, d) for d in range(1, STAGES)]
    return sum(piece.astype(f32) for piece in arrived).astype(bf16)


def relay_scatter(pieces, axes):
    half = STAGES // 2
    up = ring(pieces[2][:half], axes, 1)
    down = ring(pieces[2][half:], axes, -1)
    from_low = ring(jnp.concatenate([pieces[1][:half] + up, pieces[1][half:]]), axes, 1)
    from_high = ring(jnp.concatenate([pieces[3][:half], pieces[3][half:] + down]), axes, -1)
    total = pieces[0].astype(f32) + from_low.astype(f32) + from_high.astype(f32)
    return [row.astype(bf16) for row in total]


def per_device(inputs, cotangent, w_in, w_out, norm_gain):
    batches, tok_rows, features = inputs.shape
    own_rows, lowrank = w_in.shape[2:]
    z, yh = lax.axis_index("z"), lax.axis_index("yh")
    low = lax.rem(z, 2)
    leg = jnp.where(jnp.logical_or(z == 0, z == STAGES - 1), 0, 1)
    stage = lax.rem(STAGES - z, STAGES)
    pairs = [(i, i ^ 1) for i in range(STAGES)]

    gain = norm_gain[:, 0].astype(f32)[:, :, None]
    wide_in = w_in[:, 0].astype(f32)
    both = jnp.stack([(wide_in * gain).astype(bf16), w_out[:, 0]], 1)
    keep = lax.dynamic_index_in_dim(both, leg, 0, keepdims=False)
    other = lax.ppermute(lax.dynamic_index_in_dim(both, 1 - leg, 0, keepdims=False), "z", pairs)
    local = jnp.where(low == 0, jnp.stack([keep, other]), jnp.stack([other, keep]))
    gathered = lax.all_gather(local, PLANE, axis=0, tiled=False)
    core, x_here = lax.axis_index("c"), lax.axis_index("x")
    y_here = 2 * yh + lax.axis_index("yl")
    ticks = PARTS + 2 * STAGES - 2
    moments = jnp.arange(ticks, dtype=jnp.int32)

    def rows_for(part, first):
        active = jnp.logical_and(part >= 0, part < PARTS)
        fixed = jnp.stack([leg, first, yh]).astype(jnp.int32)
        moving = jnp.stack([active.astype(jnp.int32), jnp.clip(part, 0, PARTS - 1)], 1)
        return jnp.concatenate([moving, jnp.broadcast_to(fixed, (ticks, 3))], 1)

    table = jnp.concatenate(
        [
            rows_for(moments - stage, stage == 0),
            rows_for(moments - (2 * STAGES - 2) + stage, stage == STAGES - 1),
            jnp.stack([1 - core, x_here, leg, y_here, yh])[None],
            jnp.stack([core, x_here, leg, y_here, yh])[None],
        ]
    ).astype(jnp.int32)
    weights, feed, cot, coming, returning, kept_x, kept_act, kept_u, kept_h, kept_l = place(
        table, gathered, inputs, cotangent
    )
    weights = weights.reshape((2, weights.shape[0] // 2) + weights.shape[1:])

    onward = [(z_from, (z_from - 1) % STAGES) for z_from in (0, 3, 2)]
    homeward = [(b, a) for a, b in onward]
    for tick in range(ticks):
        do_forward = tick < PARTS + STAGES - 1
        do_backward = tick >= STAGES - 1
        if do_forward:
            if tick > STAGES - 1:
                coming, kept_h = lax.optimization_barrier((coming, kept_h))
            coming, kept_x, kept_act = forward_visit(tick, table, feed, coming, weights, kept_x, kept_act)
            if tick < PARTS + STAGES - 2:
                coming = lax.ppermute(coming, "z", onward)
        if do_backward:
            returning, kept_u, kept_h, kept_l = backward_visit(
                ticks + tick, table, cot, returning, weights, kept_x, kept_act, kept_u, kept_h, kept_l
            )
            if tick < PARTS + 2 * STAGES - 3:
                returning = lax.ppermute(returning, "z", homeward)

    def reduced(wide, thin, along_x):
        theirs = lax.ppermute(
            weight_grads(2 * ticks, table, wide, thin, own_rows, along_x), "c", [(0, 1), (1, 0)]
        )
        ours = weight_grads(2 * ticks + 1, table, wide, thin, own_rows, along_x)
        sums = [(ours[d].astype(f32) + theirs[d].astype(f32)).astype(bf16) for d in range(STAGES)]
        order = ("x", ("yh", "yl")) if along_x else (("yh", "yl"), "x")
        return ring_scatter(relay_scatter(sums, order[0]), order[1])

    owned = jnp.stack([reduced(kept_x, kept_h, True), reduced(kept_u, kept_l, False)], 1)
    kept = lax.dynamic_index_in_dim(owned, low, 0, keepdims=False)
    swapped = lax.ppermute(lax.dynamic_index_in_dim(owned, 1 - low, 0, keepdims=False), "z", pairs)
    legs = jnp.where(leg == 0, jnp.stack([kept, swapped]), jnp.stack([swapped, kept])).astype(f32)
    grad_in = legs[:, 0] * gain
    gain_grad = jnp.sum(legs[:, 0] * wide_in, axis=-1)
    return grad_in[:, None], legs[:, 1][:, None], gain_grad[:, None]


def solution(mesh):
    fine = Mesh(mesh.devices.reshape(STAGES, 2, 2, 4, 2), ("z",) + PLANE)
    sec, dp = ("z", "yh"), ("yl", "x", "c")
    return jax.shard_map(
        per_device,
        mesh=fine,
        in_specs=(
            P(None, dp, None),
            P(None, dp, None),
            P(None, sec, dp, None),
            P(None, sec, dp, None),
            P(None, sec, dp),
        ),
        out_specs=(
            P(None, sec, dp, None),
            P(None, sec, dp, None),
            P(None, sec, dp),
        ),
        check_vma=False,
    )
```

```python
import functools

import jax
import jax.numpy as jnp
from jax import lax
from jax.experimental import pallas as pl
from jax.experimental.pallas import tpu as pltpu
from jax.sharding import Mesh, PartitionSpec as P

EPS = 1e-06
PARTS = 2
STAGES = 4
DEPTH = 4
PLANE = ("yh", "yl", "x", "c")
bf16, f32 = jnp.bfloat16, jnp.float32


def narrow_t(left, right):
    return lax.dot_general(left, right, (((1,), (1,)), ((), ())), preferred_element_type=f32)


def square_mean_inverse(rows):
    return lax.rsqrt(jnp.mean(rows * rows, axis=-1, keepdims=True) + EPS)


def layer_weights(weights, layer, side):
    width = weights.shape[1] * weights.shape[-2]
    return weights[lax.rem(layer, 2), :, layer // 2, side].reshape(width, weights.shape[-1])


def forward_kernel(
    table, feed, incoming, weights, _, __, outgoing, kept_x, kept_act, stage_x, sems, *, row
):
    info = [table[row, i] for i in range(4)]

    @pl.when(info[0] == 1)
    def _run():
        part = info[1]

        def keep(place):
            return pltpu.make_async_copy(stage_x.at[place], kept_x.at[part, place], sems.at[place])

        xs = jnp.where(info[3] == 1, feed[part], incoming[...]).astype(f32)
        for place in range(DEPTH):
            layer = layer_of(info, place)
            rows = xs.astype(bf16)
            stage_x[place] = rows
            keep(place).start()
            inv = square_mean_inverse(rows.astype(f32))
            act = jnp.dot(rows, layer_weights(weights, layer, 0), preferred_element_type=f32) * inv
            kept_act[part, place] = act
            lifted = (act * jax.nn.sigmoid(act)).astype(bf16)
            xs = xs + narrow_t(lifted, layer_weights(weights, layer, 1))
        outgoing[...] = xs.astype(bf16)
        for place in range(DEPTH):
            keep(place).wait()


def backward_kernel(
    table, feed, incoming, weights, kept_x, kept_act, _, __, ___, outgoing, kept_u, kept_h, kept_l,
    stage_x, stage_u, sems, *, row,
):
    info = [table[row, i] for i in range(4)]

    @pl.when(info[0] == 1)
    def _run():
        part = info[1]

        def fetch(place):
            return pltpu.make_async_copy(kept_x.at[part, place], stage_x.at[place], sems.at[0, place])

        def keep(place):
            return pltpu.make_async_copy(stage_u.at[place], kept_u.at[part, place], sems.at[1, place])

        for place in reversed(range(DEPTH)):
            fetch(place).start()
        us = jnp.where(info[3] == 1, feed[part], incoming[...]).astype(f32)
        for place in reversed(range(DEPTH)):
            layer = layer_of(info, place)
            rows = us.astype(bf16)
            stage_u[place] = rows
            keep(place).start()
            grad_lift = jnp.dot(rows, layer_weights(weights, layer, 1), preferred_element_type=f32)
            act = kept_act[part, place]
            fetch(place).wait()
            entered = stage_x[place].astype(f32)
            inv = square_mean_inverse(entered)
            logistic = jax.nn.sigmoid(act)
            grad_act = grad_lift * logistic * (1.0 + act * (1.0 - logistic))
            scaled = (grad_act * inv).astype(bf16)
            kept_h[part, place] = scaled
            kept_l[part, place] = (act * logistic).astype(bf16)
            weight = jnp.sum(grad_act * act, axis=-1, keepdims=True) * (inv * inv) * (1.0 / us.shape[1])
            us = us + narrow_t(scaled, layer_weights(weights, layer, 0)) - entered * weight
        outgoing[...] = us.astype(bf16)
        for place in range(DEPTH):
            keep(place).wait()


def grads_kernel(table, wide, thin, out, *, along_x, row):
    info = [table[row, i] for i in range(4)]
    parts, _, rows, _ = wide.shape
    lowrank = thin.shape[-1]
    chips, _, lows, block, _ = out.shape

    def one(at, _):
        outer, inner, low = at // (chips * lows), lax.rem(at // lows, chips), lax.rem(at, lows)
        dx, dy = (outer, inner) if along_x else (inner, outer)
        x, y = lax.rem(info[1] + dx, chips), lax.rem(info[3] + dy, chips)
        place = layer_of(info, lows * low + y // 2)
        column = pl.multiple_of(((lax.rem(y, 2) * chips + x) * 2 + info[0]) * block, block)
        left = wide[:, place, :, pl.ds(column, block)].reshape(parts * rows, block)
        right = thin[:, place].reshape(parts * rows, lowrank)
        made = lax.dot_general(left, right, (((0,), (0,)), ((), ())), preferred_element_type=f32)
        out[outer, inner, low] = made.astype(bf16)
        return 0

    lax.fori_loop(0, chips * chips * lows, one, 0, unroll=16)


def layer_of(info, place):
    return jnp.where(info[2] == 0, place, DEPTH - 1 - place)


SM = pl.BlockSpec(memory_space=pltpu.SMEM)
VM = pl.BlockSpec(memory_space=pltpu.VMEM)
ANY = pl.BlockSpec(memory_space=pl.ANY)
LIMIT = 12 * 1024 * 1024


def shape_of(array):
    return jax.ShapeDtypeStruct(array.shape, array.dtype)


def cost_of(rows, weights):
    flops = 2 * rows * weights.size
    return pl.CostEstimate(flops=flops, bytes_accessed=weights.size * 4, transcendentals=0)


def staged(rows, width):
    return pltpu.VMEM((DEPTH, rows, width), bf16)


def first_kernel(
    table, source, inputs, cotangent, weights, feed, cot, returning, outgoing, kept_x, kept_act, kept_u, kept_h,
    kept_l, xs, lifted, stage_x, feed_sems, weight_sems, keep_sems,
):
    info = [table[0, i] for i in range(5)]
    active, part, parts = info[0] == 1, info[1], feed.shape[0]
    start, half = info[4] * parts, weights.shape[1] // 2
    fed = [
        pltpu.make_async_copy(inputs.at[pl.ds(start, parts)], feed, feed_sems.at[0]),
        pltpu.make_async_copy(cotangent.at[pl.ds(start, parts)], cot, feed_sems.at[1]),
    ]

    def moves(place, side):
        layer = layer_of(info, place)
        yh, zl = lax.rem(layer, 2), layer // 2
        for piece in range(2):
            spot = (yh, pl.ds(piece * half, half), zl, side)
            yield pltpu.make_async_copy(source.at[spot], weights.at[spot], weight_sems.at[place, side, piece])

    def keep(place):
        return pltpu.make_async_copy(stage_x.at[place], kept_x.at[part, place], keep_sems.at[place])

    fed[0].start()
    for place in range(DEPTH):
        for side in range(2):
            for copy in moves(place, side):
                copy.start()
    fed[1].start()
    fed[0].wait()

    @pl.when(active)
    def _load():
        xs[...] = feed[part].astype(f32)

    for place in range(DEPTH):
        layer = layer_of(info, place)
        for copy in moves(place, 0):
            copy.wait()

        @pl.when(active)
        def _in(place=place, layer=layer):
            rows = xs[...].astype(bf16)
            stage_x[place] = rows
            keep(place).start()
            inv = square_mean_inverse(rows.astype(f32))
            act = jnp.dot(rows, layer_weights(weights, layer, 0), preferred_element_type=f32) * inv
            kept_act[part, place] = act
            lifted[...] = (act * jax.nn.sigmoid(act)).astype(bf16)

        for copy in moves(place, 1):
            copy.wait()

        @pl.when(active)
        def _out(layer=layer):
            xs[...] = xs[...] + narrow_t(lifted[...], layer_weights(weights, layer, 1))

    fed[1].wait()

    @pl.when(active)
    def _store():
        outgoing[...] = xs[...].astype(bf16)
        for place in range(DEPTH):
            keep(place).wait()


def first_visit(table, source, inputs, cotangent):
    rows, width = inputs.shape[1:]
    lowrank = source.shape[-1]
    fed = jax.ShapeDtypeStruct((PARTS, rows, width), bf16)
    stream = jax.ShapeDtypeStruct((rows, width), bf16)
    wide = jax.ShapeDtypeStruct((PARTS, DEPTH, rows, width), bf16)
    thin = jax.ShapeDtypeStruct((PARTS, DEPTH, rows, lowrank), bf16)
    acts = jax.ShapeDtypeStruct((PARTS, DEPTH, rows, lowrank), f32)
    shapes = [shape_of(source), fed, fed, stream, stream, wide, acts, wide, thin, thin]
    return pl.pallas_call(
        first_kernel,
        in_specs=[SM, ANY, ANY, ANY],
        out_specs=[VM] * len(shapes),
        out_shape=shapes,
        scratch_shapes=[
            pltpu.VMEM((rows, width), f32),
            pltpu.VMEM((rows, lowrank), bf16),
            staged(rows, width),
            pltpu.SemaphoreType.DMA((2,)),
            pltpu.SemaphoreType.DMA((DEPTH, 2, 2)),
            pltpu.SemaphoreType.DMA((DEPTH,)),
        ],
        compiler_params=pltpu.CompilerParams(vmem_limit_bytes=LIMIT),
        cost_estimate=pl.CostEstimate(flops=2 * rows * source.size, bytes_accessed=source.size * 4, transcendentals=0),
        name="first_visit",
    )(table, source, inputs, cotangent)


def forward_visit(row, table, feed, incoming, weights, kept_x, kept_act):
    return pl.pallas_call(
        functools.partial(forward_kernel, row=row),
        in_specs=[SM, VM, VM, VM, VM, VM],
        out_specs=[VM, VM, VM],
        scratch_shapes=[staged(*incoming.shape), pltpu.SemaphoreType.DMA((DEPTH,))],
        out_shape=[shape_of(incoming), shape_of(kept_x), shape_of(kept_act)],
        input_output_aliases={4: 1, 5: 2},
        compiler_params=pltpu.CompilerParams(vmem_limit_bytes=LIMIT),
        cost_estimate=cost_of(incoming.shape[0], weights),
        name="forward_visit",
    )(table, feed, incoming, weights, kept_x, kept_act)


def backward_visit(row, table, feed, incoming, weights, kept_x, kept_act, kept_u, kept_h, kept_l):
    return pl.pallas_call(
        functools.partial(backward_kernel, row=row),
        in_specs=[SM, VM, VM, VM, VM, VM, VM, VM, VM],
        out_specs=[VM, VM, VM, VM],
        scratch_shapes=[staged(*incoming.shape), staged(*incoming.shape), pltpu.SemaphoreType.DMA((2, DEPTH))],
        out_shape=[shape_of(incoming), shape_of(kept_u), shape_of(kept_h), shape_of(kept_l)],
        input_output_aliases={6: 1, 7: 2, 8: 3},
        compiler_params=pltpu.CompilerParams(vmem_limit_bytes=LIMIT),
        cost_estimate=cost_of(incoming.shape[0], weights),
        name="backward_visit",
    )(table, feed, incoming, weights, kept_x, kept_act, kept_u, kept_h, kept_l)


def weight_grads(row, table, wide, thin, block, along_x):
    shape = (STAGES, STAGES, 2, block, thin.shape[-1])
    flops = 2 * wide.size // DEPTH * thin.shape[-1] * 2
    return pl.pallas_call(
        functools.partial(grads_kernel, along_x=along_x, row=row),
        in_specs=[SM, VM, VM],
        out_specs=VM,
        out_shape=jax.ShapeDtypeStruct(shape, bf16),
        compiler_params=pltpu.CompilerParams(vmem_limit_bytes=LIMIT),
        cost_estimate=pl.CostEstimate(flops=flops, bytes_accessed=wide.size * 4, transcendentals=0),
        name="grads_x" if along_x else "grads_y",
    )(table, wide, thin)


def ring(value, axes, steps):
    return lax.ppermute(value, axes, [(i, (i + steps) % STAGES) for i in range(STAGES)])


def ring_scatter(pieces, axes):
    arrived = [pieces[0]] + [ring(pieces[d], axes, d) for d in range(1, STAGES)]
    return sum(piece.astype(f32) for piece in arrived).astype(bf16)


def relay_scatter(pieces, axes):
    half = STAGES // 2
    up = ring(pieces[2][:half], axes, 1)
    down = ring(pieces[2][half:], axes, -1)
    from_low = ring(jnp.concatenate([pieces[1][:half] + up, pieces[1][half:]]), axes, 1)
    from_high = ring(jnp.concatenate([pieces[3][:half], pieces[3][half:] + down]), axes, -1)
    total = pieces[0].astype(f32) + from_low.astype(f32) + from_high.astype(f32)
    return [row.astype(bf16) for row in total]


def per_device(inputs, cotangent, w_in, w_out, norm_gain):
    batches, tok_rows, features = inputs.shape
    own_rows, lowrank = w_in.shape[2:]
    z, yh = lax.axis_index("z"), lax.axis_index("yh")
    low = lax.rem(z, 2)
    leg = jnp.where(jnp.logical_or(z == 0, z == STAGES - 1), 0, 1)
    stage = lax.rem(STAGES - z, STAGES)
    pairs = [(i, i ^ 1) for i in range(STAGES)]

    gain = norm_gain[:, 0].astype(f32)[:, :, None]
    wide_in = w_in[:, 0].astype(f32)
    both = jnp.stack([(wide_in * gain).astype(bf16), w_out[:, 0]], 1)
    keep = lax.dynamic_index_in_dim(both, leg, 0, keepdims=False)
    other = lax.ppermute(lax.dynamic_index_in_dim(both, 1 - leg, 0, keepdims=False), "z", pairs)
    local = jnp.where(low == 0, jnp.stack([keep, other]), jnp.stack([other, keep]))
    gathered = lax.all_gather(local, PLANE, axis=0, tiled=False)
    core, x_here = lax.axis_index("c"), lax.axis_index("x")
    y_here = 2 * yh + lax.axis_index("yl")
    ticks = PARTS + 2 * STAGES - 2
    moments = jnp.arange(ticks, dtype=jnp.int32)

    def rows_for(part, first):
        active = jnp.logical_and(part >= 0, part < PARTS)
        fixed = jnp.stack([leg, first, yh]).astype(jnp.int32)
        moving = jnp.stack([active.astype(jnp.int32), jnp.clip(part, 0, PARTS - 1)], 1)
        return jnp.concatenate([moving, jnp.broadcast_to(fixed, (ticks, 3))], 1)

    table = jnp.concatenate(
        [
            rows_for(moments - stage, stage == 0),
            rows_for(moments - (2 * STAGES - 2) + stage, stage == STAGES - 1),
            jnp.stack([1 - core, x_here, leg, y_here, yh])[None],
            jnp.stack([core, x_here, leg, y_here, yh])[None],
        ]
    ).astype(jnp.int32)
    gathered = gathered.reshape((2, gathered.shape[0] // 2) + gathered.shape[1:])
    weights, feed, cot, returning, coming, kept_x, kept_act, kept_u, kept_h, kept_l = first_visit(
        table, gathered, inputs, cotangent
    )

    onward = [(z_from, (z_from - 1) % STAGES) for z_from in (0, 3, 2)]
    homeward = [(b, a) for a, b in onward]
    for tick in range(ticks):
        do_forward = tick < PARTS + STAGES - 1
        do_backward = tick >= STAGES - 1
        if do_forward:
            if tick > STAGES - 1:
                coming, kept_h = lax.optimization_barrier((coming, kept_h))
            if tick > 0:
                coming, kept_x, kept_act = forward_visit(tick, table, feed, coming, weights, kept_x, kept_act)
            if tick < PARTS + STAGES - 2:
                coming = lax.ppermute(coming, "z", onward)
        if do_backward:
            returning, kept_u, kept_h, kept_l = backward_visit(
                ticks + tick, table, cot, returning, weights, kept_x, kept_act, kept_u, kept_h, kept_l
            )
            if tick < PARTS + 2 * STAGES - 3:
                returning = lax.ppermute(returning, "z", homeward)

    def reduced(wide, thin, along_x):
        theirs = lax.ppermute(
            weight_grads(2 * ticks, table, wide, thin, own_rows, along_x), "c", [(0, 1), (1, 0)]
        )
        ours = weight_grads(2 * ticks + 1, table, wide, thin, own_rows, along_x)
        sums = [(ours[d].astype(f32) + theirs[d].astype(f32)).astype(bf16) for d in range(STAGES)]
        order = ("x", ("yh", "yl")) if along_x else (("yh", "yl"), "x")
        return ring_scatter(relay_scatter(sums, order[0]), order[1])

    owned = jnp.stack([reduced(kept_x, kept_h, True), reduced(kept_u, kept_l, False)], 1)
    kept = lax.dynamic_index_in_dim(owned, low, 0, keepdims=False)
    swapped = lax.ppermute(lax.dynamic_index_in_dim(owned, 1 - low, 0, keepdims=False), "z", pairs)
    legs = jnp.where(leg == 0, jnp.stack([kept, swapped]), jnp.stack([swapped, kept])).astype(f32)
    grad_in = legs[:, 0] * gain
    gain_grad = jnp.sum(legs[:, 0] * wide_in, axis=-1)
    return grad_in[:, None], legs[:, 1][:, None], gain_grad[:, None]


def solution(mesh):
    fine = Mesh(mesh.devices.reshape(STAGES, 2, 2, 4, 2), ("z",) + PLANE)
    sec, dp = ("z", "yh"), ("yl", "x", "c")
    return jax.shard_map(
        per_device,
        mesh=fine,
        in_specs=(
            P(None, dp, None),
            P(None, dp, None),
            P(None, sec, dp, None),
            P(None, sec, dp, None),
            P(None, sec, dp),
        ),
        out_specs=(
            P(None, sec, dp, None),
            P(None, sec, dp, None),
            P(None, sec, dp),
        ),
        check_vma=False,
    )
```

```python
import functools

import jax
import jax.numpy as jnp
from jax import lax
from jax.experimental import pallas as pl
from jax.experimental.pallas import tpu as pltpu
from jax.sharding import Mesh, PartitionSpec as P

EPS = 1e-06
PARTS = 2
STAGES = 4
DEPTH = 4
PLANE = ("yh", "yl", "x", "c")
bf16, f32 = jnp.bfloat16, jnp.float32


def narrow_t(left, right):
    return lax.dot_general(left, right, (((1,), (1,)), ((), ())), preferred_element_type=f32)


def square_mean_inverse(rows):
    return lax.rsqrt(jnp.mean(rows * rows, axis=-1, keepdims=True) + EPS)


def layer_weights(weights, layer, side):
    width = weights.shape[1] * weights.shape[-2]
    return weights[lax.rem(layer, 2), :, layer // 2, side].reshape(width, weights.shape[-1])


def forward_kernel(
    table, feed, incoming, weights, _, __, outgoing, kept_x, kept_act, stage_x, sems, *, row
):
    info = [table[row, i] for i in range(4)]

    @pl.when(info[0] == 1)
    def _run():
        part = info[1]

        def keep(place):
            return pltpu.make_async_copy(stage_x.at[place], kept_x.at[part, place], sems.at[place])

        xs = jnp.where(info[3] == 1, feed[part], incoming[...]).astype(f32)
        for place in range(DEPTH):
            layer = layer_of(info, place)
            rows = xs.astype(bf16)
            stage_x[place] = rows
            keep(place).start()
            inv = square_mean_inverse(rows.astype(f32))
            act = jnp.dot(rows, layer_weights(weights, layer, 0), preferred_element_type=f32) * inv
            kept_act[part, place] = act
            lifted = (act * jax.nn.sigmoid(act)).astype(bf16)
            xs = xs + narrow_t(lifted, layer_weights(weights, layer, 1))
        outgoing[...] = xs.astype(bf16)
        for place in range(DEPTH):
            keep(place).wait()


def backward_kernel(
    table, feed, incoming, weights, kept_x, kept_act, _, __, ___, outgoing, kept_u, kept_h, kept_l,
    stage_x, stage_u, sems, *, row,
):
    info = [table[row, i] for i in range(4)]

    @pl.when(info[0] == 1)
    def _run():
        part = info[1]

        def fetch(place):
            return pltpu.make_async_copy(kept_x.at[part, place], stage_x.at[place], sems.at[0, place])

        def keep(place):
            return pltpu.make_async_copy(stage_u.at[place], kept_u.at[part, place], sems.at[1, place])

        for place in reversed(range(DEPTH)):
            fetch(place).start()
        us = jnp.where(info[3] == 1, feed[part], incoming[...]).astype(f32)
        for place in reversed(range(DEPTH)):
            layer = layer_of(info, place)
            rows = us.astype(bf16)
            stage_u[place] = rows
            keep(place).start()
            grad_lift = jnp.dot(rows, layer_weights(weights, layer, 1), preferred_element_type=f32)
            act = kept_act[part, place]
            fetch(place).wait()
            entered = stage_x[place].astype(f32)
            inv = square_mean_inverse(entered)
            logistic = jax.nn.sigmoid(act)
            grad_act = grad_lift * logistic * (1.0 + act * (1.0 - logistic))
            scaled = (grad_act * inv).astype(bf16)
            kept_h[part, place] = scaled
            kept_l[part, place] = (act * logistic).astype(bf16)
            weight = jnp.sum(grad_act * act, axis=-1, keepdims=True) * (inv * inv) * (1.0 / us.shape[1])
            us = us + narrow_t(scaled, layer_weights(weights, layer, 0)) - entered * weight
        outgoing[...] = us.astype(bf16)
        for place in range(DEPTH):
            keep(place).wait()


def pack_kernel(table, kept_x, kept_u, kept_h, kept_l, wide, thin, *, row, part):
    block = thin.shape[-1]
    for side, (broad, narrow) in enumerate(((kept_x, kept_h), (kept_u, kept_l))):
        for place in range(DEPTH):
            thin[side, place] = narrow[part, place]
            for spot in range(wide.shape[-1] // block):
                column = pl.multiple_of((2 * spot + table[row, 0]) * block, block)
                wide[side, place, :, spot * block : (spot + 1) * block] = broad[part, place, :, pl.ds(column, block)]


def grads_kernel(table, wide, thin, *rest, along_x, row):
    outs, got = rest[-STAGES:], rest[:-STAGES]
    side = 0 if along_x else 1
    info = [table[row, i] for i in range(4)]
    parts, _, rows, _ = wide.shape
    lowrank = thin.shape[-1]
    chips, lows, block, _ = outs[0].shape

    for outer, out in enumerate(outs):

        def one(at, _, outer=outer, out=out):
            inner, low = at // lows, lax.rem(at, lows)
            dx, dy = (outer, inner) if along_x else (inner, outer)
            x, y = lax.rem(info[1] + dx, chips), lax.rem(info[3] + dy, chips)
            place = layer_of(info, lows * low + y // 2)
            spot = lax.rem(y, 2) * chips + x
            column = pl.multiple_of((spot * 2 + info[0]) * block, block)
            packed = pl.multiple_of(spot * block, block)
            left = [wide[:, place, :, pl.ds(column, block)].reshape(parts * rows, block)]
            right = [thin[:, place].reshape(parts * rows, lowrank)]
            left += [broad[side, place, :, pl.ds(packed, block)] for broad in got[::2]]
            right += [narrow[side, place] for narrow in got[1::2]]
            made = lax.dot_general(
                jnp.concatenate(left), jnp.concatenate(right), (((0,), (0,)), ((), ())), preferred_element_type=f32
            )
            out[inner, low] = made.astype(bf16)
            return 0

        lax.fori_loop(0, chips * lows, one, 0, unroll=8)


def layer_of(info, place):
    return jnp.where(info[2] == 0, place, DEPTH - 1 - place)


SM = pl.BlockSpec(memory_space=pltpu.SMEM)
VM = pl.BlockSpec(memory_space=pltpu.VMEM)
ANY = pl.BlockSpec(memory_space=pl.ANY)
LIMIT = 12 * 1024 * 1024


def shape_of(array):
    return jax.ShapeDtypeStruct(array.shape, array.dtype)


def cost_of(rows, weights):
    flops = 2 * rows * weights.size
    return pl.CostEstimate(flops=flops, bytes_accessed=weights.size * 4, transcendentals=0)


def staged(rows, width):
    return pltpu.VMEM((DEPTH, rows, width), bf16)


def first_kernel(
    table, source, inputs, cotangent, weights, feed, cot, returning, outgoing, kept_x, kept_act, kept_u, kept_h,
    kept_l, xs, lifted, stage_x, feed_sems, weight_sems, keep_sems,
):
    info = [table[0, i] for i in range(5)]
    active, part, parts = info[0] == 1, info[1], feed.shape[0]
    start, half = info[4] * parts, weights.shape[1] // 2
    fed = [
        pltpu.make_async_copy(inputs.at[pl.ds(start, parts)], feed, feed_sems.at[0]),
        pltpu.make_async_copy(cotangent.at[pl.ds(start, parts)], cot, feed_sems.at[1]),
    ]

    def moves(place, side):
        layer = layer_of(info, place)
        yh, zl = lax.rem(layer, 2), layer // 2
        for piece in range(2):
            spot = (yh, pl.ds(piece * half, half), zl, side)
            yield pltpu.make_async_copy(source.at[spot], weights.at[spot], weight_sems.at[place, side, piece])

    def keep(place):
        return pltpu.make_async_copy(stage_x.at[place], kept_x.at[part, place], keep_sems.at[place])

    fed[0].start()
    for place in range(DEPTH):
        for side in range(2):
            for copy in moves(place, side):
                copy.start()
    fed[1].start()
    fed[0].wait()

    @pl.when(active)
    def _load():
        xs[...] = feed[part].astype(f32)

    for place in range(DEPTH):
        layer = layer_of(info, place)
        for copy in moves(place, 0):
            copy.wait()

        @pl.when(active)
        def _in(place=place, layer=layer):
            rows = xs[...].astype(bf16)
            stage_x[place] = rows
            keep(place).start()
            inv = square_mean_inverse(rows.astype(f32))
            act = jnp.dot(rows, layer_weights(weights, layer, 0), preferred_element_type=f32) * inv
            kept_act[part, place] = act
            lifted[...] = (act * jax.nn.sigmoid(act)).astype(bf16)

        for copy in moves(place, 1):
            copy.wait()

        @pl.when(active)
        def _out(layer=layer):
            xs[...] = xs[...] + narrow_t(lifted[...], layer_weights(weights, layer, 1))

    fed[1].wait()

    @pl.when(active)
    def _store():
        outgoing[...] = xs[...].astype(bf16)
        for place in range(DEPTH):
            keep(place).wait()


def first_visit(table, source, inputs, cotangent):
    rows, width = inputs.shape[1:]
    lowrank = source.shape[-1]
    fed = jax.ShapeDtypeStruct((PARTS, rows, width), bf16)
    stream = jax.ShapeDtypeStruct((rows, width), bf16)
    wide = jax.ShapeDtypeStruct((PARTS, DEPTH, rows, width), bf16)
    thin = jax.ShapeDtypeStruct((PARTS, DEPTH, rows, lowrank), bf16)
    acts = jax.ShapeDtypeStruct((PARTS, DEPTH, rows, lowrank), f32)
    shapes = [shape_of(source), fed, fed, stream, stream, wide, acts, wide, thin, thin]
    return pl.pallas_call(
        first_kernel,
        in_specs=[SM, ANY, ANY, ANY],
        out_specs=[VM] * len(shapes),
        out_shape=shapes,
        scratch_shapes=[
            pltpu.VMEM((rows, width), f32),
            pltpu.VMEM((rows, lowrank), bf16),
            staged(rows, width),
            pltpu.SemaphoreType.DMA((2,)),
            pltpu.SemaphoreType.DMA((DEPTH, 2, 2)),
            pltpu.SemaphoreType.DMA((DEPTH,)),
        ],
        compiler_params=pltpu.CompilerParams(vmem_limit_bytes=LIMIT),
        cost_estimate=pl.CostEstimate(flops=2 * rows * source.size, bytes_accessed=source.size * 4, transcendentals=0),
        name="first_visit",
    )(table, source, inputs, cotangent)


def forward_visit(row, table, feed, incoming, weights, kept_x, kept_act):
    return pl.pallas_call(
        functools.partial(forward_kernel, row=row),
        in_specs=[SM, VM, VM, VM, VM, VM],
        out_specs=[VM, VM, VM],
        scratch_shapes=[staged(*incoming.shape), pltpu.SemaphoreType.DMA((DEPTH,))],
        out_shape=[shape_of(incoming), shape_of(kept_x), shape_of(kept_act)],
        input_output_aliases={4: 1, 5: 2},
        compiler_params=pltpu.CompilerParams(vmem_limit_bytes=LIMIT),
        cost_estimate=cost_of(incoming.shape[0], weights),
        name="forward_visit",
    )(table, feed, incoming, weights, kept_x, kept_act)


def backward_visit(row, table, feed, incoming, weights, kept_x, kept_act, kept_u, kept_h, kept_l):
    return pl.pallas_call(
        functools.partial(backward_kernel, row=row),
        in_specs=[SM, VM, VM, VM, VM, VM, VM, VM, VM],
        out_specs=[VM, VM, VM, VM],
        scratch_shapes=[staged(*incoming.shape), staged(*incoming.shape), pltpu.SemaphoreType.DMA((2, DEPTH))],
        out_shape=[shape_of(incoming), shape_of(kept_u), shape_of(kept_h), shape_of(kept_l)],
        input_output_aliases={6: 1, 7: 2, 8: 3},
        compiler_params=pltpu.CompilerParams(vmem_limit_bytes=LIMIT),
        cost_estimate=cost_of(incoming.shape[0], weights),
        name="backward_visit",
    )(table, feed, incoming, weights, kept_x, kept_act, kept_u, kept_h, kept_l)


def pack(row, table, part, kept_x, kept_u, kept_h, kept_l):
    _, depth, rows, width = kept_x.shape
    shapes = [
        jax.ShapeDtypeStruct((2, depth, rows, width // 2), bf16),
        jax.ShapeDtypeStruct((2, depth, rows, kept_h.shape[-1]), bf16),
    ]
    packed = pl.pallas_call(
        functools.partial(pack_kernel, row=row, part=part),
        in_specs=[SM] + [VM] * 4,
        out_specs=[VM] * 2,
        out_shape=shapes,
        compiler_params=pltpu.CompilerParams(vmem_limit_bytes=LIMIT),
        name="pack",
    )(table, kept_x, kept_u, kept_h, kept_l)
    return packed


def across(arrays):
    return [lax.ppermute(array, "c", [(0, 1), (1, 0)]) for array in arrays]


def weight_grads(row, table, wide, thin, got, block, along_x):
    shape = jax.ShapeDtypeStruct((STAGES, 2, block, thin.shape[-1]), bf16)
    flops = 2 * wide.size // DEPTH * thin.shape[-1] * 4
    return pl.pallas_call(
        functools.partial(grads_kernel, along_x=along_x, row=row),
        in_specs=[SM] + [VM] * (2 + len(got)),
        out_specs=[VM] * STAGES,
        out_shape=[shape] * STAGES,
        compiler_params=pltpu.CompilerParams(vmem_limit_bytes=LIMIT),
        cost_estimate=pl.CostEstimate(flops=flops, bytes_accessed=wide.size * 4, transcendentals=0),
        name="grads_x" if along_x else "grads_y",
    )(table, wide, thin, *got)


def ring(value, axes, steps):
    return lax.ppermute(value, axes, [(i, (i + steps) % STAGES) for i in range(STAGES)])


def ring_scatter(pieces, axes):
    arrived = [pieces[0]] + [ring(pieces[d], axes, d) for d in range(1, STAGES)]
    return sum(piece.astype(f32) for piece in arrived).astype(bf16)


def add_kernel(piece, extra, out, *, start):
    stop = start + extra.shape[0]
    out[start:stop] = (piece[start:stop].astype(f32) + extra[...].astype(f32)).astype(bf16)


def add_part(piece, extra, start):
    return pl.pallas_call(
        functools.partial(add_kernel, start=start),
        in_specs=[VM] * 2,
        out_specs=VM,
        out_shape=shape_of(piece),
        input_output_aliases={0: 0},
        compiler_params=pltpu.CompilerParams(vmem_limit_bytes=LIMIT),
        name="add_part",
    )(piece, extra)


def sum_kernel(own, below, above, *outs):
    for i, out in enumerate(outs):
        out[...] = (own[i].astype(f32) + below[i].astype(f32) + above[i].astype(f32)).astype(bf16)


def relay_scatter(pieces, axes):
    half = STAGES // 2
    up = ring(pieces[2][:half], axes, 1)
    down = ring(pieces[2][half:], axes, -1)
    from_low = ring(add_part(pieces[1], up, 0), axes, 1)
    from_high = ring(add_part(pieces[3], down, half), axes, -1)
    return pl.pallas_call(
        sum_kernel,
        in_specs=[VM] * 3,
        out_specs=[VM] * STAGES,
        out_shape=[jax.ShapeDtypeStruct(pieces[0].shape[1:], bf16)] * STAGES,
        compiler_params=pltpu.CompilerParams(vmem_limit_bytes=LIMIT),
        name="sum_parts",
    )(pieces[0], from_low, from_high)


def fold_kernel(leg, w_in, w_out, gains, keep, send):
    for out, which in ((keep, leg[0]), (send, 1 - leg[0])):
        gain = jnp.where(which == 0, gains[0:1], gains[1:2]).astype(f32)
        column = jnp.broadcast_to(gain, w_in.shape[1:]).T
        out[0] = (w_in[which].astype(f32) * column).astype(bf16)
        out[1] = w_out[which]


def fold(leg, w_in, w_out, gains):
    shape = jax.ShapeDtypeStruct(w_in.shape, bf16)
    return pl.pallas_call(
        fold_kernel,
        in_specs=[SM, VM, VM, VM],
        out_specs=[VM, VM],
        out_shape=[shape, shape],
        compiler_params=pltpu.CompilerParams(vmem_limit_bytes=LIMIT),
        name="fold",
    )(leg, w_in, w_out, gains)


def per_device(inputs, cotangent, w_in, w_out, norm_gain):
    batches, tok_rows, features = inputs.shape
    own_rows, lowrank = w_in.shape[2:]
    z, yh = lax.axis_index("z"), lax.axis_index("yh")
    low = lax.rem(z, 2)
    leg = jnp.where(jnp.logical_or(z == 0, z == STAGES - 1), 0, 1)
    stage = lax.rem(STAGES - z, STAGES)
    pairs = [(i, i ^ 1) for i in range(STAGES)]

    gain = norm_gain[:, 0].astype(f32)[:, :, None]
    wide_in = w_in[:, 0].astype(f32)
    keep, send = fold(leg[None].astype(jnp.int32), w_in[:, 0], w_out[:, 0], norm_gain[:, 0])
    other = lax.ppermute(send, "z", pairs)
    local = jnp.where(low == 0, jnp.stack([keep, other]), jnp.stack([other, keep]))
    gathered = lax.all_gather(local, PLANE, axis=0, tiled=False)
    core, x_here = lax.axis_index("c"), lax.axis_index("x")
    y_here = 2 * yh + lax.axis_index("yl")
    ticks = PARTS + 2 * STAGES - 2
    moments = jnp.arange(ticks, dtype=jnp.int32)

    def rows_for(part, first):
        active = jnp.logical_and(part >= 0, part < PARTS)
        fixed = jnp.stack([leg, first, yh]).astype(jnp.int32)
        moving = jnp.stack([active.astype(jnp.int32), jnp.clip(part, 0, PARTS - 1)], 1)
        return jnp.concatenate([moving, jnp.broadcast_to(fixed, (ticks, 3))], 1)

    table = jnp.concatenate(
        [
            rows_for(moments - stage, stage == 0),
            rows_for(moments - (2 * STAGES - 2) + stage, stage == STAGES - 1),
            jnp.stack([1 - core, x_here, leg, y_here, yh])[None],
            jnp.stack([core, x_here, leg, y_here, yh])[None],
        ]
    ).astype(jnp.int32)
    gathered = gathered.reshape((2, gathered.shape[0] // 2) + gathered.shape[1:])
    weights, feed, cot, returning, coming, kept_x, kept_act, kept_u, kept_h, kept_l = first_visit(
        table, gathered, inputs, cotangent
    )

    onward = [(z_from, (z_from - 1) % STAGES) for z_from in (0, 3, 2)]
    homeward = [(b, a) for a, b in onward]
    got = []
    for tick in range(ticks):
        do_forward = tick < PARTS + STAGES - 1
        do_backward = tick >= STAGES - 1
        if do_forward:
            if tick > STAGES - 1:
                coming, kept_h = lax.optimization_barrier((coming, kept_h))
            if tick > 0:
                coming, kept_x, kept_act = forward_visit(tick, table, feed, coming, weights, kept_x, kept_act)
            if tick < PARTS + STAGES - 2:
                coming = lax.ppermute(coming, "z", onward)
        if do_backward:
            if tick == ticks - 1:
                for part in range(PARTS - 1):
                    early = pack(2 * ticks, table, part, kept_x, kept_u, kept_h, kept_l)
                    returning, early = lax.optimization_barrier((returning, early))
                    got += across(early)
            returning, kept_u, kept_h, kept_l = backward_visit(
                ticks + tick, table, cot, returning, weights, kept_x, kept_act, kept_u, kept_h, kept_l
            )
            if tick < PARTS + 2 * STAGES - 3:
                returning = lax.ppermute(returning, "z", homeward)

    got += across(pack(2 * ticks, table, PARTS - 1, kept_x, kept_u, kept_h, kept_l))

    def reduced(wide, thin, along_x):
        sums = weight_grads(2 * ticks + 1, table, wide, thin, got, own_rows, along_x)
        order = ("x", ("yh", "yl")) if along_x else (("yh", "yl"), "x")
        return ring_scatter(relay_scatter(sums, order[0]), order[1])

    owned = jnp.stack([reduced(kept_x, kept_h, True), reduced(kept_u, kept_l, False)], 1)
    kept = lax.dynamic_index_in_dim(owned, low, 0, keepdims=False)
    swapped = lax.ppermute(lax.dynamic_index_in_dim(owned, 1 - low, 0, keepdims=False), "z", pairs)
    legs = jnp.where(leg == 0, jnp.stack([kept, swapped]), jnp.stack([swapped, kept])).astype(f32)
    grad_in = legs[:, 0] * gain
    gain_grad = jnp.sum(legs[:, 0] * wide_in, axis=-1)
    return grad_in[:, None], legs[:, 1][:, None], gain_grad[:, None]


def solution(mesh):
    fine = Mesh(mesh.devices.reshape(STAGES, 2, 2, 4, 2), ("z",) + PLANE)
    sec, dp = ("z", "yh"), ("yl", "x", "c")
    return jax.shard_map(
        per_device,
        mesh=fine,
        in_specs=(
            P(None, dp, None),
            P(None, dp, None),
            P(None, sec, dp, None),
            P(None, sec, dp, None),
            P(None, sec, dp),
        ),
        out_specs=(
            P(None, sec, dp, None),
            P(None, sec, dp, None),
            P(None, sec, dp),
        ),
        check_vma=False,
    )
```

```python
import functools

import jax
import jax.numpy as jnp
from jax import lax
from jax.experimental import pallas as pl
from jax.experimental.pallas import tpu as pltpu
from jax.sharding import Mesh, PartitionSpec as P

EPS = 1e-06
PARTS = 2
STAGES = 4
DEPTH = 4
PLANE = ("yh", "yl", "x", "c")
bf16, f32 = jnp.bfloat16, jnp.float32


def narrow_t(left, right):
    return lax.dot_general(left, right, (((1,), (1,)), ((), ())), preferred_element_type=f32)


def square_mean_inverse(rows):
    return lax.rsqrt(jnp.mean(rows * rows, axis=-1, keepdims=True) + EPS)


def layer_weights(weights, layer, side):
    width = weights.shape[1] * weights.shape[-2]
    return weights[lax.rem(layer, 2), :, layer // 2, side].reshape(width, weights.shape[-1])


def forward_kernel(
    table, feed, incoming, weights, _, __, outgoing, kept_x, kept_act, stage_x, sems, *, row, last
):
    info = [table[row, i] for i in range(4)]

    @pl.when(info[0] == 1)
    def _run():
        part = info[1]

        def keep(place):
            return pltpu.make_async_copy(stage_x.at[place], kept_x.at[part, place], sems.at[place])

        xs = jnp.where(info[3] == 1, feed[part], incoming[...]).astype(f32)
        for place in range(DEPTH):
            layer = layer_of(info, place)
            rows = xs.astype(bf16)
            stage_x[place] = rows
            keep(place).start()
            inv = square_mean_inverse(rows.astype(f32))
            act = jnp.dot(rows, layer_weights(weights, layer, 0), preferred_element_type=f32) * inv
            kept_act[part, place] = act
            lifted = (act * jax.nn.sigmoid(act)).astype(bf16)
            xs = xs + narrow_t(lifted, layer_weights(weights, layer, 1))
        if not last:
            outgoing[...] = xs.astype(bf16)
        for place in range(DEPTH):
            keep(place).wait()


def backward_kernel(
    table, feed, incoming, weights, kept_x, kept_act, _, __, ___, outgoing, kept_u, kept_h, kept_l,
    stage_x, stage_u, sems, *, row, last,
):
    info = [table[row, i] for i in range(4)]

    @pl.when(info[0] == 1)
    def _run():
        part = info[1]

        def fetch(place):
            return pltpu.make_async_copy(kept_x.at[part, place], stage_x.at[place], sems.at[0, place])

        def keep(place):
            return pltpu.make_async_copy(stage_u.at[place], kept_u.at[part, place], sems.at[1, place])

        for place in reversed(range(DEPTH)):
            fetch(place).start()
        us = jnp.where(info[3] == 1, feed[part], incoming[...]).astype(f32)
        for place in reversed(range(DEPTH)):
            layer = layer_of(info, place)
            rows = us.astype(bf16)
            stage_u[place] = rows
            keep(place).start()
            grad_lift = jnp.dot(rows, layer_weights(weights, layer, 1), preferred_element_type=f32)
            act = kept_act[part, place]
            fetch(place).wait()
            entered = stage_x[place].astype(f32)
            inv = square_mean_inverse(entered)
            logistic = jax.nn.sigmoid(act)
            grad_act = grad_lift * logistic * (1.0 + act * (1.0 - logistic))
            scaled = (grad_act * inv).astype(bf16)
            kept_h[part, place] = scaled
            kept_l[part, place] = (act * logistic).astype(bf16)
            weight = jnp.sum(grad_act * act, axis=-1, keepdims=True) * (inv * inv) * (1.0 / us.shape[1])
            us = us + narrow_t(scaled, layer_weights(weights, layer, 0)) - entered * weight
        if not last:
            outgoing[...] = us.astype(bf16)
        for place in range(DEPTH):
            keep(place).wait()


def pack_kernel(table, kept_x, kept_u, kept_h, kept_l, wide, thin, *, row, part):
    block = thin.shape[-1]
    for side, (broad, narrow) in enumerate(((kept_x, kept_h), (kept_u, kept_l))):
        for place in range(DEPTH):
            thin[side, place] = narrow[part, place]
            for spot in range(wide.shape[-1] // block):
                column = pl.multiple_of((2 * spot + table[row, 0]) * block, block)
                wide[side, place, :, spot * block : (spot + 1) * block] = broad[part, place, :, pl.ds(column, block)]


def grads_kernel(table, wide, thin, *rest, along_x, row):
    outs, got = rest[-STAGES:], rest[:-STAGES]
    side = 0 if along_x else 1
    info = [table[row, i] for i in range(4)]
    parts, _, rows, _ = wide.shape
    lowrank = thin.shape[-1]
    chips, lows, block, _ = outs[0].shape

    for outer, out in enumerate(outs):

        def one(at, _, outer=outer, out=out):
            inner, low = at // lows, lax.rem(at, lows)
            dx, dy = (outer, inner) if along_x else (inner, outer)
            x, y = lax.rem(info[1] + dx, chips), lax.rem(info[3] + dy, chips)
            place = layer_of(info, lows * low + y // 2)
            spot = lax.rem(y, 2) * chips + x
            column = pl.multiple_of((spot * 2 + info[0]) * block, block)
            packed = pl.multiple_of(spot * block, block)
            left = [wide[:, place, :, pl.ds(column, block)].reshape(parts * rows, block)]
            right = [thin[:, place].reshape(parts * rows, lowrank)]
            left += [broad[side, place, :, pl.ds(packed, block)] for broad in got[::2]]
            right += [narrow[side, place] for narrow in got[1::2]]
            made = lax.dot_general(
                jnp.concatenate(left), jnp.concatenate(right), (((0,), (0,)), ((), ())), preferred_element_type=f32
            )
            out[inner, low] = made.astype(bf16)
            return 0

        lax.fori_loop(0, chips * lows, one, 0, unroll=8)


def layer_of(info, place):
    return jnp.where(info[2] == 0, place, DEPTH - 1 - place)


SM = pl.BlockSpec(memory_space=pltpu.SMEM)
VM = pl.BlockSpec(memory_space=pltpu.VMEM)
ANY = pl.BlockSpec(memory_space=pl.ANY)
LIMIT = 12 * 1024 * 1024


def shape_of(array):
    return jax.ShapeDtypeStruct(array.shape, array.dtype)


def cost_of(rows, weights):
    flops = 2 * rows * weights.size
    return pl.CostEstimate(flops=flops, bytes_accessed=weights.size * 4, transcendentals=0)


def staged(rows, width):
    return pltpu.VMEM((DEPTH, rows, width), bf16)


def first_kernel(
    table, source, inputs, cotangent, weights, feed, cot, returning, outgoing, kept_x, kept_act, kept_u, kept_h,
    kept_l, xs, lifted, stage_x, feed_sems, weight_sems, keep_sems,
):
    info = [table[0, i] for i in range(5)]
    active, part, parts = info[0] == 1, info[1], feed.shape[0]
    start, half = info[4] * parts, weights.shape[1] // 2
    fed = [
        pltpu.make_async_copy(inputs.at[pl.ds(start, parts)], feed, feed_sems.at[0]),
        pltpu.make_async_copy(cotangent.at[pl.ds(start, parts)], cot, feed_sems.at[1]),
    ]

    def moves(place, side):
        layer = layer_of(info, place)
        yh, zl = lax.rem(layer, 2), layer // 2
        for piece in range(2):
            spot = (yh, pl.ds(piece * half, half), zl, side)
            yield pltpu.make_async_copy(source.at[spot], weights.at[spot], weight_sems.at[place, side, piece])

    def keep(place):
        return pltpu.make_async_copy(stage_x.at[place], kept_x.at[part, place], keep_sems.at[place])

    fed[0].start()
    for place in range(DEPTH):
        for side in range(2):
            for copy in moves(place, side):
                copy.start()
    fed[1].start()
    fed[0].wait()

    @pl.when(active)
    def _load():
        xs[...] = feed[part].astype(f32)

    for place in range(DEPTH):
        layer = layer_of(info, place)
        for copy in moves(place, 0):
            copy.wait()

        @pl.when(active)
        def _in(place=place, layer=layer):
            rows = xs[...].astype(bf16)
            stage_x[place] = rows
            keep(place).start()
            inv = square_mean_inverse(rows.astype(f32))
            act = jnp.dot(rows, layer_weights(weights, layer, 0), preferred_element_type=f32) * inv
            kept_act[part, place] = act
            lifted[...] = (act * jax.nn.sigmoid(act)).astype(bf16)

        for copy in moves(place, 1):
            copy.wait()

        @pl.when(active)
        def _out(layer=layer):
            xs[...] = xs[...] + narrow_t(lifted[...], layer_weights(weights, layer, 1))

    fed[1].wait()

    @pl.when(active)
    def _store():
        outgoing[...] = xs[...].astype(bf16)
        for place in range(DEPTH):
            keep(place).wait()


def first_visit(table, source, inputs, cotangent):
    rows, width = inputs.shape[1:]
    lowrank = source.shape[-1]
    fed = jax.ShapeDtypeStruct((PARTS, rows, width), bf16)
    stream = jax.ShapeDtypeStruct((rows, width), bf16)
    wide = jax.ShapeDtypeStruct((PARTS, DEPTH, rows, width), bf16)
    thin = jax.ShapeDtypeStruct((PARTS, DEPTH, rows, lowrank), bf16)
    acts = jax.ShapeDtypeStruct((PARTS, DEPTH, rows, lowrank), f32)
    shapes = [shape_of(source), fed, fed, stream, stream, wide, acts, wide, thin, thin]
    return pl.pallas_call(
        first_kernel,
        in_specs=[SM, ANY, ANY, ANY],
        out_specs=[VM] * len(shapes),
        out_shape=shapes,
        scratch_shapes=[
            pltpu.VMEM((rows, width), f32),
            pltpu.VMEM((rows, lowrank), bf16),
            staged(rows, width),
            pltpu.SemaphoreType.DMA((2,)),
            pltpu.SemaphoreType.DMA((DEPTH, 2, 2)),
            pltpu.SemaphoreType.DMA((DEPTH,)),
        ],
        compiler_params=pltpu.CompilerParams(vmem_limit_bytes=LIMIT),
        cost_estimate=pl.CostEstimate(flops=2 * rows * source.size, bytes_accessed=source.size * 4, transcendentals=0),
        name="first_visit",
    )(table, source, inputs, cotangent)


def forward_visit(last, row, table, feed, incoming, weights, kept_x, kept_act):
    return pl.pallas_call(
        functools.partial(forward_kernel, row=row, last=last),
        in_specs=[SM, VM, VM, VM, VM, VM],
        out_specs=[ANY if last else VM, VM, VM],
        scratch_shapes=[staged(*incoming.shape), pltpu.SemaphoreType.DMA((DEPTH,))],
        out_shape=[shape_of(incoming), shape_of(kept_x), shape_of(kept_act)],
        input_output_aliases={4: 1, 5: 2},
        compiler_params=pltpu.CompilerParams(vmem_limit_bytes=LIMIT),
        cost_estimate=cost_of(incoming.shape[0], weights),
        name="forward_visit",
    )(table, feed, incoming, weights, kept_x, kept_act)


def backward_visit(last, row, table, feed, incoming, weights, kept_x, kept_act, kept_u, kept_h, kept_l):
    return pl.pallas_call(
        functools.partial(backward_kernel, row=row, last=last),
        in_specs=[SM, VM, VM, VM, VM, VM, VM, VM, VM],
        out_specs=[ANY if last else VM, VM, VM, VM],
        scratch_shapes=[staged(*incoming.shape), staged(*incoming.shape), pltpu.SemaphoreType.DMA((2, DEPTH))],
        out_shape=[shape_of(incoming), shape_of(kept_u), shape_of(kept_h), shape_of(kept_l)],
        input_output_aliases={6: 1, 7: 2, 8: 3},
        compiler_params=pltpu.CompilerParams(vmem_limit_bytes=LIMIT),
        cost_estimate=cost_of(incoming.shape[0], weights),
        name="backward_visit",
    )(table, feed, incoming, weights, kept_x, kept_act, kept_u, kept_h, kept_l)


def pack(row, table, part, kept_x, kept_u, kept_h, kept_l):
    _, depth, rows, width = kept_x.shape
    shapes = [
        jax.ShapeDtypeStruct((2, depth, rows, width // 2), bf16),
        jax.ShapeDtypeStruct((2, depth, rows, kept_h.shape[-1]), bf16),
    ]
    packed = pl.pallas_call(
        functools.partial(pack_kernel, row=row, part=part),
        in_specs=[SM] + [VM] * 4,
        out_specs=[VM] * 2,
        out_shape=shapes,
        compiler_params=pltpu.CompilerParams(vmem_limit_bytes=LIMIT),
        name="pack",
    )(table, kept_x, kept_u, kept_h, kept_l)
    return packed


def across(arrays):
    return [lax.ppermute(array, "c", [(0, 1), (1, 0)]) for array in arrays]


def weight_grads(row, table, wide, thin, got, block, along_x):
    shape = jax.ShapeDtypeStruct((STAGES, 2, block, thin.shape[-1]), bf16)
    flops = 2 * wide.size // DEPTH * thin.shape[-1] * 4
    return pl.pallas_call(
        functools.partial(grads_kernel, along_x=along_x, row=row),
        in_specs=[SM] + [VM] * (2 + len(got)),
        out_specs=[VM] * STAGES,
        out_shape=[shape] * STAGES,
        compiler_params=pltpu.CompilerParams(vmem_limit_bytes=LIMIT),
        cost_estimate=pl.CostEstimate(flops=flops, bytes_accessed=wide.size * 4, transcendentals=0),
        name="grads_x" if along_x else "grads_y",
    )(table, wide, thin, *got)


def ring(value, axes, steps):
    return lax.ppermute(value, axes, [(i, (i + steps) % STAGES) for i in range(STAGES)])


def ring_scatter(pieces, axes):
    arrived = [pieces[0]] + [ring(pieces[d], axes, d) for d in range(1, STAGES)]
    return sum(piece.astype(f32) for piece in arrived).astype(bf16)


def add_kernel(piece, extra, out, *, start):
    stop = start + extra.shape[0]
    out[start:stop] = (piece[start:stop].astype(f32) + extra[...].astype(f32)).astype(bf16)


def add_part(piece, extra, start):
    return pl.pallas_call(
        functools.partial(add_kernel, start=start),
        in_specs=[VM] * 2,
        out_specs=VM,
        out_shape=shape_of(piece),
        input_output_aliases={0: 0},
        compiler_params=pltpu.CompilerParams(vmem_limit_bytes=LIMIT),
        name="add_part",
    )(piece, extra)


def sum_kernel(own, below, above, *outs):
    for i, out in enumerate(outs):
        out[...] = (own[i].astype(f32) + below[i].astype(f32) + above[i].astype(f32)).astype(bf16)


def relay_scatter(pieces, axes):
    half = STAGES // 2
    up = ring(pieces[2][:half], axes, 1)
    down = ring(pieces[2][half:], axes, -1)
    from_low = ring(add_part(pieces[1], up, 0), axes, 1)
    from_high = ring(add_part(pieces[3], down, half), axes, -1)
    return pl.pallas_call(
        sum_kernel,
        in_specs=[VM] * 3,
        out_specs=[VM] * STAGES,
        out_shape=[jax.ShapeDtypeStruct(pieces[0].shape[1:], bf16)] * STAGES,
        compiler_params=pltpu.CompilerParams(vmem_limit_bytes=LIMIT),
        name="sum_parts",
    )(pieces[0], from_low, from_high)


def fold_kernel(leg, w_in, w_out, gains, keep, send):
    for out, which in ((keep, leg[0]), (send, 1 - leg[0])):
        gain = jnp.where(which == 0, gains[0:1], gains[1:2]).astype(f32)
        column = jnp.broadcast_to(gain, w_in.shape[1:]).T
        out[0] = (w_in[which].astype(f32) * column).astype(bf16)
        out[1] = w_out[which]


def fold(leg, w_in, w_out, gains):
    shape = jax.ShapeDtypeStruct(w_in.shape, bf16)
    return pl.pallas_call(
        fold_kernel,
        in_specs=[SM, VM, VM, VM],
        out_specs=[VM, VM],
        out_shape=[shape, shape],
        compiler_params=pltpu.CompilerParams(vmem_limit_bytes=LIMIT),
        name="fold",
    )(leg, w_in, w_out, gains)


def per_device(inputs, cotangent, w_in, w_out, norm_gain):
    batches, tok_rows, features = inputs.shape
    own_rows, lowrank = w_in.shape[2:]
    z, yh = lax.axis_index("z"), lax.axis_index("yh")
    low = lax.rem(z, 2)
    leg = jnp.where(jnp.logical_or(z == 0, z == STAGES - 1), 0, 1)
    stage = lax.rem(STAGES - z, STAGES)
    pairs = [(i, i ^ 1) for i in range(STAGES)]

    gain = norm_gain[:, 0].astype(f32)[:, :, None]
    wide_in = w_in[:, 0].astype(f32)
    keep, send = fold(leg[None].astype(jnp.int32), w_in[:, 0], w_out[:, 0], norm_gain[:, 0])
    other = lax.ppermute(send, "z", pairs)
    local = jnp.where(low == 0, jnp.stack([keep, other]), jnp.stack([other, keep]))
    gathered = lax.all_gather(local, PLANE, axis=0, tiled=False)
    core, x_here = lax.axis_index("c"), lax.axis_index("x")
    y_here = 2 * yh + lax.axis_index("yl")
    ticks = PARTS + 2 * STAGES - 2
    moments = jnp.arange(ticks, dtype=jnp.int32)

    def rows_for(part, first):
        active = jnp.logical_and(part >= 0, part < PARTS)
        fixed = jnp.stack([leg, first, yh]).astype(jnp.int32)
        moving = jnp.stack([active.astype(jnp.int32), jnp.clip(part, 0, PARTS - 1)], 1)
        return jnp.concatenate([moving, jnp.broadcast_to(fixed, (ticks, 3))], 1)

    table = jnp.concatenate(
        [
            rows_for(moments - stage, stage == 0),
            rows_for(moments - (2 * STAGES - 2) + stage, stage == STAGES - 1),
            jnp.stack([1 - core, x_here, leg, y_here, yh])[None],
            jnp.stack([core, x_here, leg, y_here, yh])[None],
        ]
    ).astype(jnp.int32)
    gathered = gathered.reshape((2, gathered.shape[0] // 2) + gathered.shape[1:])
    weights, feed, cot, returning, coming, kept_x, kept_act, kept_u, kept_h, kept_l = first_visit(
        table, gathered, inputs, cotangent
    )

    onward = [(z_from, (z_from - 1) % STAGES) for z_from in (0, 3, 2)]
    homeward = [(b, a) for a, b in onward]
    got = []
    for tick in range(ticks):
        do_forward = tick < PARTS + STAGES - 1
        do_backward = tick >= STAGES - 1
        if do_forward:
            if tick > STAGES - 1:
                coming, kept_h = lax.optimization_barrier((coming, kept_h))
            if tick > 0:
                coming, kept_x, kept_act = forward_visit(tick == PARTS + STAGES - 2, tick, table, feed, coming, weights, kept_x, kept_act)
            if tick < PARTS + STAGES - 2:
                coming = lax.ppermute(coming, "z", onward)
        if do_backward:
            if tick == ticks - 1:
                for part in range(PARTS - 1):
                    early = pack(2 * ticks, table, part, kept_x, kept_u, kept_h, kept_l)
                    returning, early = lax.optimization_barrier((returning, early))
                    got += across(early)
            returning, kept_u, kept_h, kept_l = backward_visit(
                tick == ticks - 1, ticks + tick, table, cot, returning, weights, kept_x, kept_act, kept_u, kept_h, kept_l
            )
            if tick < PARTS + 2 * STAGES - 3:
                returning = lax.ppermute(returning, "z", homeward)

    got += across(pack(2 * ticks, table, PARTS - 1, kept_x, kept_u, kept_h, kept_l))

    def reduced(wide, thin, along_x):
        sums = weight_grads(2 * ticks + 1, table, wide, thin, got, own_rows, along_x)
        order = ("x", ("yh", "yl")) if along_x else (("yh", "yl"), "x")
        return ring_scatter(relay_scatter(sums, order[0]), order[1])

    owned = jnp.stack([reduced(kept_x, kept_h, True), reduced(kept_u, kept_l, False)], 1)
    kept = lax.dynamic_index_in_dim(owned, low, 0, keepdims=False)
    swapped = lax.ppermute(lax.dynamic_index_in_dim(owned, 1 - low, 0, keepdims=False), "z", pairs)
    legs = jnp.where(leg == 0, jnp.stack([kept, swapped]), jnp.stack([swapped, kept])).astype(f32)
    grad_in = legs[:, 0] * gain
    gain_grad = jnp.sum(legs[:, 0] * wide_in, axis=-1)
    return grad_in[:, None], legs[:, 1][:, None], gain_grad[:, None]


def solution(mesh):
    fine = Mesh(mesh.devices.reshape(STAGES, 2, 2, 4, 2), ("z",) + PLANE)
    sec, dp = ("z", "yh"), ("yl", "x", "c")
    return jax.shard_map(
        per_device,
        mesh=fine,
        in_specs=(
            P(None, dp, None),
            P(None, dp, None),
            P(None, sec, dp, None),
            P(None, sec, dp, None),
            P(None, sec, dp),
        ),
        out_specs=(
            P(None, sec, dp, None),
            P(None, sec, dp, None),
            P(None, sec, dp),
        ),
        check_vma=False,
    )
```
